32 devices in a mesh: rows: 4 (over x, core), cols: 8 (over z, y).
Axes of the slice: x: 2, y: 2, z: 4, core: 2. Of those that a mesh axis runs over, the one named last changes fastest.
Arguments:
- search_vectors: bfloat16 [4096, 1024], P(('rows', 'cols')), may hold values from -6 to 6
- tile_values: bfloat16 [64, 64, 512], P('rows'), may hold values from -0.25 to 0.25
- block_columns: int32 [64, 8], P('rows'), may hold values from -4 to 67, as said below
Outputs:
- filtered: bfloat16 [4096, 1024], P(('rows', 'cols'))
- gram: float32 [1024, 1024], P('cols')
The draws below stay inside these ranges and needn't reach their ends.
Inputs may be any that keep to these rules, and one draw needn't show every extreme that they name: `block_columns`: row b names 8 distinct block columns, each within 4 of b, always including b - 4, b and b + 4; block columns outside 0 to 63 stand for zero tiles.
All inputs are finite; a program needn't handle non-finite values.
Results may differ from the reference program's by a relative error of at most 0.023.
Values may be sent and summed in bfloat16 or wider, within the bound.
No kernel may reach another device: no remote copies, remote signals or barrier semaphores. Data moves between devices by JAX's collectives and lax.ppermute only.
A program may use at most 64 MiB of HBM per device.

```python
import jax
import jax.numpy as jnp
from jax import lax

M = 1024
TILE = 64
KT = 8
HALO = 4
DEGREE = 8
BLK_DEV = 16
NBLK = 64
NROWS = 4096
N_ROWS = 4


def draw_block_columns(key, part):
    subkeys = jax.random.split(key, NBLK)
    inner = jnp.concatenate([jnp.arange(1 - HALO, 0), jnp.arange(1, HALO)]).astype(jnp.int32)

    def choose(subkey):
        return jax.random.permutation(subkey, inner)[:KT - 3]
    chosen = jax.vmap(choose)(subkeys)
    anchors = jnp.arange(NBLK, dtype=jnp.int32)[:, None]
    outer_offsets = jnp.broadcast_to(jnp.array([-HALO, 0, HALO], jnp.int32), (NBLK, 3))
    offsets = jnp.concatenate([outer_offsets, chosen], axis=1)
    return (anchors + offsets).astype(jnp.int32)


def levels(own_key, extent, cuts, least, high):
    gain = 1.0
    for axis_at, shards_of in cuts:
        steps = jax.random.uniform(jax.random.fold_in(jax.random.fold_in(own_key, 6), axis_at), (shards_of,), jnp.float32, least / len(cuts), high / len(cuts))
        gain = gain * jnp.repeat(jnp.exp(steps), extent[axis_at] // shards_of).reshape((-1,) + (1,) * (len(extent) - 1 - axis_at))
    return gain


def noise(stream_key, extent, scale, bound, pieces=(), kind=jnp.bfloat16):
    level = levels(stream_key, extent, pieces, -0.22, 0.18) if pieces else 1.0
    result = jax.random.normal(stream_key, extent, jnp.float32) * scale * level
    return jnp.minimum(jnp.maximum(result, -bound), bound).astype(kind)


def setup_inputs(seed: int = 0) -> dict:
    arg_keys = jax.random.split(jax.random.key(seed), 4)
    return {
        "search_vectors": noise(arg_keys[0], (NROWS, M), 1.0, 6.0, ((0, 32),)),
        "tile_values": noise(arg_keys[1], (NBLK, TILE, KT * TILE), (KT * TILE) ** -0.5, 0.25, ((0, 4),)),
        "block_columns": draw_block_columns(jax.random.fold_in(arg_keys[3], 71), 0),
    }


shift_value = 0.1
half_width = 2.0


def reference(search_vectors, tile_values, block_columns):
    grouped_tiles = tile_values.reshape(N_ROWS, BLK_DEV, TILE, KT * TILE)
    grouped_index = block_columns.reshape(N_ROWS, BLK_DEV, KT)

    def filter_step(iterate):
        rounded = iterate.astype(jnp.bfloat16)
        padded = jnp.pad(rounded.reshape(NBLK, TILE, M), ((HALO, HALO), (0, 0), (0, 0)))

        def one_group(operands):
            tile_group, index_group = operands
            picked = padded[(index_group + HALO).astype(jnp.int32)]
            picked = picked.reshape(BLK_DEV, KT * TILE, M)
            return jnp.einsum("bij,bjc->bic", tile_group.astype(jnp.float32), picked.astype(jnp.float32))

        mapped = lax.map(one_group, (grouped_tiles, grouped_index))
        product = mapped.reshape(NROWS, M)
        return (product - shift_value * iterate) / half_width

    previous = search_vectors.astype(jnp.float32)
    current = filter_step(previous)
    for degree_step in range(DEGREE - 1):
        following = 2.0 * filter_step(current) - previous
        previous, current = current, following
    filtered = current.astype(jnp.bfloat16)
    gram = lax.dot_general(filtered, filtered, (((0,), (0,)), ((), ())), preferred_element_type=jnp.float32)
    return filtered, gram * (1.0 / NROWS)
```

```python
import functools

import functools

import jax
import jax.numpy as jnp
from jax import lax
from jax.experimental import pallas as pl
from jax.experimental.pallas import tpu as pltpu
from jax.sharding import PartitionSpec as P

HALO = 4
DEGREE = 8
STAGE = 4
REACH = HALO * STAGE
TILES_REACH = REACH - HALO
SPAN = 3

shift_value = 0.1
half_width = 2.0

SMEM = pl.BlockSpec(memory_space=pltpu.SMEM)
VMEM = pl.BlockSpec(memory_space=pltpu.VMEM)


def params(mebibytes):
    return pltpu.CompilerParams(vmem_limit_bytes=mebibytes * 1024 * 1024)


def with_core(value):
    return lax.ppermute(value, "rows", [(i, i ^ 1) for i in range(lax.axis_size("rows"))])


def with_chip(value):
    odds = range(1, lax.axis_size("rows") - 1, 2)
    return lax.ppermute(value, "rows", [p for k in odds for p in ((k, k + 1), (k + 1, k))])


def place_group(offsets, ahead, tiles, start, bands, band, doubled, slot):
    kt = offsets.shape[0]
    tile = tiles.shape[1]
    blank = kt
    nothing = jnp.zeros((tile, tile), doubled.dtype)
    for i in range(HALO):
        values = tiles[start + i]
        for k in range(kt):
            one = values[:, k * tile:(k + 1) * tile]
            doubled[i, k] = jnp.concatenate([one, one], axis=1)
        for place in range(2 * HALO + 1):
            slot[i, place] = blank
        for k in range(kt):
            slot[i, offsets[k, ahead + start + i] + HALO] = k
    for i in range(HALO):
        rows = slice(i * tile, (i + 1) * tile)
        for pair in range(SPAN * HALO // 2):
            halves = []
            for side in range(2):
                place = 2 * pair + side - i
                if 0 <= place <= 2 * HALO:
                    both = doubled[i, slot[i, place]]
                    halves.append(both[:, side * tile:(side + 1) * tile])
                else:
                    halves.append(nothing)
            columns = slice(2 * pair * tile, 2 * (pair + 1) * tile)
            bands[band, rows, columns] = jnp.concatenate(halves, axis=1)


def clear(doubled):
    doubled[:, doubled.shape[1] - 1] = jnp.zeros(
        doubled.shape[:1] + doubled.shape[2:], doubled.dtype
    )


def split_columns(vectors, pieces):
    width = pieces.shape[2]
    for i in range(pieces.shape[0]):
        pieces[i] = vectors[:, i * width:(i + 1) * width]


def own_bands(odd, offsets, columns, tiles, _, bands, to_first, columns_out, doubled, slot):
    count = tiles.shape[0]
    sent = to_first.shape[0]
    to_first[...] = tiles[pl.ds((1 - odd[0]) * (count - sent), sent)]
    columns_out[...] = columns[...]
    clear(doubled)

    @pl.loop(0, count // HALO)
    def _(g):
        place_group(offsets, 0, tiles, g * HALO, bands, g, doubled, slot)


def edge_bands(odd, at_first, at_second, first, second, bands, doubled, slot):
    count = at_first.shape[1]
    edge = TILES_REACH // HALO
    clear(doubled)
    for offsets, tiles, behind in ((at_first, first, odd[0]), (at_second, second, 1 - odd[0])):
        begin = behind * (count - TILES_REACH)
        band = (1 - behind) * edge
        skipped = begin * (tiles.shape[0] // count)

        @pl.loop(0, edge)
        def _(g, offsets=offsets, tiles=tiles, begin=begin, band=band, skipped=skipped):
            place_group(offsets, begin - skipped, tiles, skipped + g * HALO, bands, band + g,
                        doubled, slot)


def run_steps(own, edges, w, y, degree):
    middle, size, span = own.shape
    edge = edges.shape[0] // 2
    bands = [edges.at[j] for j in range(edge)]
    bands += [own.at[j] for j in range(middle)]
    bands += [edges.at[edge + j] for j in range(edge)]
    groups = len(bands)
    cur, new = y
    src, dst = w
    for step in range(STAGE):
        for j in range(step, groups - step):
            start = j * size
            here = slice(start + size, start + 2 * size)
            product = dot(bands[j][...], src[start:start + span])
            value = product - shift_value * cur[here]
            value = value / half_width if degree + step == 0 else value - new[here]
            new[here] = value
            dst[here] = value.astype(jnp.bfloat16)
        cur, new = new, cur
        src, dst = dst, src
    return cur, new, src


def placed(behind, rows):
    return pl.multiple_of((1 - behind) * 2 * rows, rows)


def first_stage(odd, own, edges, x_first, x_own, x_second, now_out, last_out, sent_out,
                w0, w1, y0, y1):
    rows = x_own.shape[0]
    size = own.shape[1]
    starts = (placed(odd[0], rows), rows, placed(1 - odd[0], rows))
    for start, ref in zip(starts, (x_first, x_own, x_second)):
        w0[pl.ds(start, rows)] = ref[...]
        y0[pl.ds(start, rows)] = ref[...].astype(jnp.float32)
    cur, prev, rounded = run_steps(own, edges, (w0, w1), (y0, y1), 0)
    now_out[...] = cur[rows:2 * rows]
    last_out[...] = prev[rows - size:2 * rows + size]
    sent_out[:rows] = rounded[rows:2 * rows]
    sent_out[rows:] = prev[rows + size:2 * rows - size].astype(jnp.bfloat16)


def second_stage(odd, own, edges, now, last, got_first, got_second, out, w0, w1, y0, y1):
    rows = now.shape[0]
    size = own.shape[1]
    here = slice(rows, 2 * rows)
    w0[here] = now[...].astype(jnp.bfloat16)
    y0[here] = now[...]
    y1[rows - size:2 * rows + size] = last[...]
    for got, behind in ((got_first, odd[0]), (got_second, 1 - odd[0])):
        start = placed(behind, rows)
        w0[pl.ds(start, rows)] = got[:rows]
        y0[pl.ds(start, rows)] = got[:rows].astype(jnp.float32)
        y1[pl.ds(pl.multiple_of(start + size, size), rows - 2 * size)] = (
            got[rows:].astype(jnp.float32)
        )
    _, _, rounded = run_steps(own, edges, (w0, w1), (y0, y1), STAGE)
    out[...] = rounded[here]


def dot(a, b):
    return jnp.dot(a, b, preferred_element_type=jnp.float32)


def columns_at(ref, group, width):
    if len(ref.shape) == 2:
        return slice(None), pl.ds(pl.multiple_of(group * width, width), width)
    return (group,)


def whole(chunk):
    low, high = chunk
    return jnp.concatenate([low[...], high[...]], axis=0)


def in_pairs(chunks):
    return [chunks[t:t + 2] for t in range(0, len(chunks), 2)]


def early_gram(mine, *refs):
    *chunks, partial, lefts = refs
    half = mine.shape[0] // 2
    left = mine[...].T
    lefts[0] = left
    for t, chunk in enumerate([(mine.at[:half], mine.at[half:])] + in_pairs(chunks)):
        block = whole(chunk)
        if t:
            lefts[t] = block.T
        partial[t] = dot(left, block)


def rows_of(chunk, device, share, put):
    low, high = chunk
    half = low.shape[0]
    start = pl.multiple_of(device * share, share)

    @pl.when(start < half)
    def _():
        put(low[pl.ds(start, share)])

    @pl.when(start >= half)
    def _():
        put(high[pl.ds(start - half, share)])


def late_gram(where, lefts, *refs):
    back, front = refs[:2], refs[2:4]
    partial, *messages = refs[4:]
    width = partial.shape[1]
    share = messages[0].shape[0] - width
    reach = lefts.shape[0] // 2 + 1
    far_back, far_front = whole(back), whole(front)
    partial[0] = dot(lefts[0], far_back)
    partial[1] = dot(lefts[0], far_front)
    made = []
    for t in range(1, reach):
        made.append((dot(lefts[2 * t], far_back), back, where[2 * t]))
        made.append((dot(lefts[2 * t - 1], far_front), front, where[2 * t - 1]))
    made.append((dot(far_back.T, far_front), front, where[2 * reach - 1]))
    for message, (block, chunk, device) in zip(messages, made):
        message[:width] = block.astype(message.dtype)

        def put(rows, message=message):
            message[width:] = rows

        rows_of(chunk, device, share, put)


def assemble(where, early, late, *refs):
    *messages, partial = refs
    width = early.shape[1]
    held = early.shape[0]
    blocks = [early[t] for t in range(held)] + [late[0], late[1]]
    blocks += [message[:width].astype(jnp.float32) for message in messages]
    for t, block in enumerate(blocks):
        partial[columns_at(partial, where[t], width)] = block


def filtered_rows(number, where, mine, *refs):
    chunks, messages, rowwise = refs[:number], refs[number:-1], refs[-1]
    rows, width = mine.shape
    half = rows // 2
    share = rowwise.shape[-2]
    for t, chunk in enumerate([(mine.at[:half], mine.at[half:])] + in_pairs(chunks)):

        def put(rows, t=t):
            rowwise[columns_at(rowwise, where[t], width)] = rows

        rows_of(chunk, where[0], share, put)
    for t, message in enumerate(messages):
        at = columns_at(rowwise, where[1 + number // 2 + t], width)
        rowwise[at] = message[width:]


def ring_of(size):
    return list(range(0, size, 2)) + list(range(size - 1, 0, -2))


def gram_and_rows(mine):
    size = lax.axis_size("cols")
    device = lax.axis_index("cols")
    assert size % 4 == 0
    reach = size // 4
    order = ring_of(size)
    rows, width = mine.shape
    half = rows // 2
    share = rows // size

    def move(value, by):
        return lax.ppermute(
            value, "cols", [(order[i], order[(i + by) % size]) for i in range(size)]
        )

    low_ahead = low_behind = mine[:half]
    high_ahead = high_behind = mine[half:]
    chunks, steps = [], [0]
    for t in range(1, reach + 1):
        low_ahead, high_behind = move(low_ahead, 1), move(high_behind, -1)
        high_ahead, low_behind = move(high_ahead, 1), move(low_behind, -1)
        chunks += [low_ahead, high_ahead, low_behind, high_behind]
        steps += [-t, t]
    sends = [by for t in range(1, reach) for by in (t, -t)] + [-reach]
    steps += [-(by + reach) if by > 0 else reach - by for by in sends]

    place = jnp.where(device % 2 == 0, device // 2, size - 1 - device // 2)
    where = (place + jnp.array(steps, jnp.int32)) % size
    where = jnp.where(where < size // 2, 2 * where, 2 * (size - 1 - where) + 1)

    held = 2 * reach - 1
    early, lefts = pl.pallas_call(
        early_gram,
        out_shape=(
            jax.ShapeDtypeStruct((held, width, width), jnp.float32),
            jax.ShapeDtypeStruct((held, width, rows), mine.dtype),
        ),
        in_specs=[VMEM] * (1 + 4 * (reach - 1)),
        out_specs=(VMEM, VMEM),
        compiler_params=params(16),
    )(mine, *chunks[:-4])
    message = jax.ShapeDtypeStruct((width + share, width), mine.dtype)
    late, *messages = pl.pallas_call(
        late_gram,
        out_shape=(jax.ShapeDtypeStruct((2, width, width), jnp.float32),)
        + (message,) * len(sends),
        in_specs=[SMEM] + [VMEM] * 5,
        out_specs=(VMEM,) * (1 + len(sends)),
        compiler_params=params(16),
    )(where, lefts, *chunks[-4:])
    messages = [move(value, by) for value, by in zip(messages, sends)]

    flat = width % 128 == 0
    shape = (lambda n: (n, size * width)) if flat else (lambda n: (size, n, width))
    partial = pl.pallas_call(
        assemble,
        out_shape=jax.ShapeDtypeStruct(shape(width), jnp.float32),
        in_specs=[SMEM] + [VMEM] * (2 + len(messages)),
        out_specs=VMEM,
        compiler_params=params(16),
    )(where, early, late, *messages)
    rowwise = pl.pallas_call(
        functools.partial(filtered_rows, len(chunks)),
        out_shape=jax.ShapeDtypeStruct(shape(share), mine.dtype),
        in_specs=[SMEM] + [VMEM] * (1 + len(chunks) + len(messages)),
        out_specs=VMEM,
        compiler_params=params(16),
    )(where, mine, *chunks, *messages)
    if not flat:
        partial = partial.transpose(1, 0, 2).reshape(width, size * width)
        rowwise = rowwise.transpose(1, 0, 2).reshape(share, size * width)
    return partial, rowwise


def sum_over_rows(partial):
    size = lax.axis_size("rows")
    me = lax.axis_index("rows")
    half = partial.shape[0] // 2
    odd = me & 1
    partner = [(i, i ^ 1) for i in range(size)]
    halves = partial.reshape(2, half, partial.shape[1])
    keep = lax.dynamic_index_in_dim(halves, odd, 0, keepdims=False)
    give = lax.dynamic_index_in_dim(halves, 1 - odd, 0, keepdims=False)
    total = keep + lax.ppermute(give, "rows", partner)
    bit = 2
    while bit < size:
        sent = total.astype(jnp.bfloat16)
        got = lax.ppermute(sent, "rows", [(i, i ^ bit) for i in range(size)])
        total = sent.astype(jnp.float32) + got.astype(jnp.float32)
        bit *= 2
    other = lax.ppermute(total, "rows", partner)
    low = jnp.where(odd == 0, total, other)
    high = jnp.where(odd == 0, other, total)
    return jnp.concatenate([low, high], axis=0)


def per_device(search_vectors, tile_values, block_columns):
    row_part = lax.axis_index("rows")
    row_parts = lax.axis_size("rows")
    col_parts = lax.axis_size("cols")
    count, tile, depth = tile_values.shape
    kt = block_columns.shape[1]
    assert REACH == count
    share = search_vectors.shape[0]
    width = search_vectors.shape[1] // col_parts
    rows = share * col_parts
    second = with_chip(tile_values)
    pieces = pl.pallas_call(
        split_columns,
        out_shape=jax.ShapeDtypeStruct((col_parts, share, width), search_vectors.dtype),
        in_specs=[VMEM],
        out_specs=VMEM,
        compiler_params=params(4),
    )(search_vectors)
    columns = lax.all_to_all(pieces, "cols", split_axis=0, concat_axis=0, tiled=True)
    columns = columns.reshape(rows, width)

    size = HALO * tile
    odd = row_part & 1
    block_columns = block_columns.T
    inner = jnp.arange(count, dtype=jnp.int32)

    def offsets_of(columns, part):
        return jnp.clip(columns - (part * count + inner), -HALO, HALO)

    scratch = [
        pltpu.VMEM((HALO, kt + 1, tile, 2 * tile), jnp.bfloat16),
        pltpu.SMEM((HALO, 2 * HALO + 1), jnp.int32),
    ]
    bands, to_first, sent_columns = pl.pallas_call(
        own_bands,
        out_shape=(
            jax.ShapeDtypeStruct((count // HALO, size, SPAN * size), jnp.bfloat16),
            jax.ShapeDtypeStruct((TILES_REACH, tile, depth), jnp.bfloat16),
            jax.ShapeDtypeStruct((kt, count), jnp.int32),
        ),
        in_specs=[SMEM, SMEM, VMEM, VMEM, pl.BlockSpec(memory_space=pl.ANY)],
        out_specs=(VMEM,) * 3,
        scratch_shapes=scratch,
        compiler_params=params(16),
    )(odd[None], offsets_of(block_columns, row_part), block_columns, tile_values, pieces)
    first = with_core(to_first)
    at_first = with_core(sent_columns)
    at_second = with_chip(sent_columns)
    edges = pl.pallas_call(
        edge_bands,
        out_shape=jax.ShapeDtypeStruct(
            (2 * TILES_REACH // HALO, size, SPAN * size), jnp.bfloat16
        ),
        in_specs=[SMEM] * 3 + [VMEM] * 2,
        out_specs=VMEM,
        scratch_shapes=scratch,
        compiler_params=params(16),
    )(
        odd[None],
        offsets_of(at_first, row_part ^ 1),
        offsets_of(at_second, row_part - 1 + 2 * odd),
        first,
        second,
    )
    x_second = with_chip(columns)
    x_first = with_core(columns)

    window = [
        pltpu.VMEM((3 * rows, width), dtype)
        for dtype in (jnp.bfloat16, jnp.bfloat16, jnp.float32, jnp.float32)
    ]
    now, last, sent = pl.pallas_call(
        first_stage,
        out_shape=(
            jax.ShapeDtypeStruct((rows, width), jnp.float32),
            jax.ShapeDtypeStruct((rows + 2 * size, width), jnp.float32),
            jax.ShapeDtypeStruct((2 * rows - 2 * size, width), jnp.bfloat16),
        ),
        in_specs=[SMEM] + [VMEM] * 5,
        out_specs=(VMEM,) * 3,
        scratch_shapes=window,
        compiler_params=params(24),
    )(odd[None], bands, edges, x_first, columns, x_second)
    got_second = with_chip(sent)
    got_first = with_core(sent)
    filtered = pl.pallas_call(
        second_stage,
        out_shape=jax.ShapeDtypeStruct((rows, width), jnp.bfloat16),
        in_specs=[SMEM] + [VMEM] * 6,
        out_specs=VMEM,
        scratch_shapes=window,
        compiler_params=params(24),
    )(odd[None], bands, edges, now, last, got_first, got_second)

    partial, rowwise = gram_and_rows(filtered)
    gram = sum_over_rows(partial)
    return rowwise, gram * (1.0 / (rows * row_parts))


def solution(mesh):
    return jax.shard_map(
        per_device,
        mesh=mesh,
        in_specs=(P(("rows", "cols"), None), P("rows", None, None), P("rows", None)),
        out_specs=(P(("rows", "cols"), None), P("cols", None)),
        check_vma=False,
    )
```

```python
import functools

import functools

import jax
import jax.numpy as jnp
from jax import lax
from jax.experimental import pallas as pl
from jax.experimental.pallas import tpu as pltpu
from jax.sharding import PartitionSpec as P

HALO = 4
DEGREE = 8
STAGE = 4
REACH = HALO * STAGE
TILES_REACH = REACH - HALO
SPAN = 3

shift_value = 0.1
half_width = 2.0

SMEM = pl.BlockSpec(memory_space=pltpu.SMEM)
VMEM = pl.BlockSpec(memory_space=pltpu.VMEM)


def params(mebibytes):
    return pltpu.CompilerParams(vmem_limit_bytes=mebibytes * 1024 * 1024)


def with_core(value):
    return lax.ppermute(value, "rows", [(i, i ^ 1) for i in range(lax.axis_size("rows"))])


def with_chip(value):
    odds = range(1, lax.axis_size("rows") - 1, 2)
    return lax.ppermute(value, "rows", [p for k in odds for p in ((k, k + 1), (k + 1, k))])


def place_group(offsets, ahead, tiles, start, bands, band, doubled, slot):
    kt = offsets.shape[0]
    tile = tiles.shape[1]
    blank = kt
    nothing = jnp.zeros((tile, tile), doubled.dtype)
    for i in range(HALO):
        values = tiles[start + i]
        for k in range(kt):
            one = values[:, k * tile:(k + 1) * tile]
            doubled[i, k] = jnp.concatenate([one, one], axis=1)
        for place in range(2 * HALO + 1):
            slot[i, place] = blank
        for k in range(kt):
            slot[i, offsets[k, ahead + start + i] + HALO] = k
    for i in range(HALO):
        rows = slice(i * tile, (i + 1) * tile)
        for pair in range(SPAN * HALO // 2):
            halves = []
            for side in range(2):
                place = 2 * pair + side - i
                if 0 <= place <= 2 * HALO:
                    both = doubled[i, slot[i, place]]
                    halves.append(both[:, side * tile:(side + 1) * tile])
                else:
                    halves.append(nothing)
            columns = slice(2 * pair * tile, 2 * (pair + 1) * tile)
            bands[band, rows, columns] = jnp.concatenate(halves, axis=1)


def clear(doubled):
    doubled[:, doubled.shape[1] - 1] = jnp.zeros(
        doubled.shape[:1] + doubled.shape[2:], doubled.dtype
    )


def split_columns(vectors, pieces):
    width = pieces.shape[2]
    for i in range(pieces.shape[0]):
        pieces[i] = vectors[:, i * width:(i + 1) * width]


def own_bands(odd, offsets, columns, tiles, _, bands, to_first, columns_out, doubled, slot):
    count = tiles.shape[0]
    sent = to_first.shape[0]
    to_first[...] = tiles[pl.ds((1 - odd[0]) * (count - sent), sent)]
    columns_out[...] = columns[...]
    clear(doubled)

    @pl.loop(0, count // HALO)
    def _(g):
        place_group(offsets, 0, tiles, g * HALO, bands, g, doubled, slot)


def edge_bands(odd, at_first, at_second, first, second, bands, doubled, slot):
    count = at_first.shape[1]
    edge = TILES_REACH // HALO
    clear(doubled)
    for offsets, tiles, behind in ((at_first, first, odd[0]), (at_second, second, 1 - odd[0])):
        begin = behind * (count - TILES_REACH)
        band = (1 - behind) * edge
        skipped = begin * (tiles.shape[0] // count)

        @pl.loop(0, edge)
        def _(g, offsets=offsets, tiles=tiles, begin=begin, band=band, skipped=skipped):
            place_group(offsets, begin - skipped, tiles, skipped + g * HALO, bands, band + g,
                        doubled, slot)


def run_steps(own, edges, w, y, degree):
    middle, size, span = own.shape
    edge = edges.shape[0] // 2
    bands = [edges.at[j] for j in range(edge)]
    bands += [own.at[j] for j in range(middle)]
    bands += [edges.at[edge + j] for j in range(edge)]
    groups = len(bands)
    cur, new = y
    src, dst = w
    for step in range(STAGE):
        for j in range(step, groups - step):
            start = j * size
            here = slice(start + size, start + 2 * size)
            product = dot(bands[j][...], src[start:start + span])
            value = product - shift_value * cur[here]
            value = value / half_width if degree + step == 0 else value - new[here]
            new[here] = value
            dst[here] = value.astype(jnp.bfloat16)
        cur, new = new, cur
        src, dst = dst, src
    return cur, new, src


def placed(behind, rows):
    return pl.multiple_of((1 - behind) * 2 * rows, rows)


def first_stage(odd, own, edges, x_first, x_own, x_second, now_out, last_out, sent_out,
                w0, w1, y0, y1):
    rows = x_own.shape[0]
    size = own.shape[1]
    starts = (placed(odd[0], rows), rows, placed(1 - odd[0], rows))
    for start, ref in zip(starts, (x_first, x_own, x_second)):
        w0[pl.ds(start, rows)] = ref[...]
        y0[pl.ds(start, rows)] = ref[...].astype(jnp.float32)
    cur, prev, rounded = run_steps(own, edges, (w0, w1), (y0, y1), 0)
    now_out[...] = cur[rows:2 * rows]
    last_out[...] = prev[rows - size:2 * rows + size]
    sent_out[:rows] = rounded[rows:2 * rows]
    sent_out[rows:] = prev[rows + size:2 * rows - size].astype(jnp.bfloat16)


def second_stage(odd, own, edges, now, last, got_first, got_second, out, w0, w1, y0, y1):
    rows = now.shape[0]
    size = own.shape[1]
    here = slice(rows, 2 * rows)
    w0[here] = now[...].astype(jnp.bfloat16)
    y0[here] = now[...]
    y1[rows - size:2 * rows + size] = last[...]
    for got, behind in ((got_first, odd[0]), (got_second, 1 - odd[0])):
        start = placed(behind, rows)
        w0[pl.ds(start, rows)] = got[:rows]
        y0[pl.ds(start, rows)] = got[:rows].astype(jnp.float32)
        y1[pl.ds(pl.multiple_of(start + size, size), rows - 2 * size)] = (
            got[rows:].astype(jnp.float32)
        )
    _, _, rounded = run_steps(own, edges, (w0, w1), (y0, y1), STAGE)
    out[...] = rounded[here]


def dot(a, b):
    return jnp.dot(a, b, preferred_element_type=jnp.float32)


def columns_at(ref, group, width):
    if len(ref.shape) == 2:
        return slice(None), pl.ds(pl.multiple_of(group * width, width), width)
    return (group,)


def whole(chunk):
    low, high = chunk
    return jnp.concatenate([low[...], high[...]], axis=0)


def in_pairs(chunks):
    return [chunks[t:t + 2] for t in range(0, len(chunks), 2)]


def early_gram(mine, *refs):
    *chunks, partial, lefts = refs
    half = mine.shape[0] // 2
    left = mine[...].T
    lefts[0] = left
    for t, chunk in enumerate([(mine.at[:half], mine.at[half:])] + in_pairs(chunks)):
        block = whole(chunk)
        if t:
            lefts[t] = block.T
        partial[t] = dot(left, block)


def rows_of(chunk, device, share, put):
    low, high = chunk
    half = low.shape[0]
    start = pl.multiple_of(device * share, share)

    @pl.when(start < half)
    def _():
        put(low[pl.ds(start, share)])

    @pl.when(start >= half)
    def _():
        put(high[pl.ds(start - half, share)])


def late_gram(where, lefts, early, *refs):
    back, front = refs[:2], refs[2:4]
    partial, *messages = refs[4:]
    width = partial.shape[1]
    share = messages[0].shape[0] - width
    reach = lefts.shape[0] // 2 + 1
    far_back, far_front = whole(back), whole(front)
    partial[:2 * reach - 1] = early[...]
    partial[2 * reach - 1] = dot(lefts[0], far_back)
    partial[2 * reach] = dot(lefts[0], far_front)
    made = []
    for t in range(1, reach):
        made.append((dot(lefts[2 * t], far_back), back, where[2 * t]))
        made.append((dot(lefts[2 * t - 1], far_front), front, where[2 * t - 1]))
    made.append((dot(far_back.T, far_front), front, where[2 * reach - 1]))
    for message, (block, chunk, device) in zip(messages, made):
        message[:width] = block.astype(message.dtype)

        def put(rows, message=message):
            message[width:] = rows

        rows_of(chunk, device, share, put)


def place_blocks(scale, where, odd, *refs):
    own, own_other, far, far_other, gram = refs
    half, width = own.shape[1:]
    first = own.shape[0]
    for side, (near, distant) in enumerate(((own, far), (own_other, far_other))):
        rows = pl.ds(pl.multiple_of((odd[0] ^ side) * half, half), half)
        for t in range(first + far.shape[0]):
            block = near[t] if t < first else distant[t - first]
            if len(gram.shape) == 2:
                start = pl.multiple_of(where[t] * width, width)
                gram[rows, pl.ds(start, width)] = block * scale
            else:
                gram[where[t], rows] = block * scale


def filtered_rows(number, where, mine, *refs):
    chunks, messages, rowwise = refs[:number], refs[number:-1], refs[-1]
    rows, width = mine.shape
    half = rows // 2
    share = rowwise.shape[-2]
    for t, chunk in enumerate([(mine.at[:half], mine.at[half:])] + in_pairs(chunks)):

        def put(rows, t=t):
            rowwise[columns_at(rowwise, where[t], width)] = rows

        rows_of(chunk, where[0], share, put)
    for t, message in enumerate(messages):
        at = columns_at(rowwise, where[1 + number // 2 + t], width)
        rowwise[at] = message[width:]


def ring_of(size):
    return list(range(0, size, 2)) + list(range(size - 1, 0, -2))


def gram_and_rows(mine):
    size = lax.axis_size("cols")
    device = lax.axis_index("cols")
    assert size % 4 == 0
    reach = size // 4
    order = ring_of(size)
    rows, width = mine.shape
    half = rows // 2
    share = rows // size

    def move(value, by):
        return lax.ppermute(
            value, "cols", [(order[i], order[(i + by) % size]) for i in range(size)]
        )

    low_ahead = low_behind = mine[:half]
    high_ahead = high_behind = mine[half:]
    chunks, steps = [], [0]
    for t in range(1, reach + 1):
        low_ahead, high_behind = move(low_ahead, 1), move(high_behind, -1)
        high_ahead, low_behind = move(high_ahead, 1), move(low_behind, -1)
        chunks += [low_ahead, high_ahead, low_behind, high_behind]
        steps += [-t, t]
    sends = [by for t in range(1, reach) for by in (t, -t)] + [-reach]
    steps += [-(by + reach) if by > 0 else reach - by for by in sends]

    place = jnp.where(device % 2 == 0, device // 2, size - 1 - device // 2)
    where = (place + jnp.array(steps, jnp.int32)) % size
    where = jnp.where(where < size // 2, 2 * where, 2 * (size - 1 - where) + 1)

    held = 2 * reach - 1
    early, lefts = pl.pallas_call(
        early_gram,
        out_shape=(
            jax.ShapeDtypeStruct((held, width, width), jnp.float32),
            jax.ShapeDtypeStruct((held, width, rows), mine.dtype),
        ),
        in_specs=[VMEM] * (1 + 4 * (reach - 1)),
        out_specs=(VMEM, VMEM),
        compiler_params=params(16),
    )(mine, *chunks[:-4])
    message = jax.ShapeDtypeStruct((width + share, width), mine.dtype)
    own, *messages = pl.pallas_call(
        late_gram,
        out_shape=(jax.ShapeDtypeStruct((held + 2, width, width), jnp.float32),)
        + (message,) * len(sends),
        in_specs=[SMEM] + [VMEM] * 6,
        out_specs=(VMEM,) * (1 + len(sends)),
        compiler_params=params(16),
    )(where, lefts, early, *chunks[-4:])
    messages = [move(value, by) for value, by in zip(messages, sends)]
    own, messages = lax.optimization_barrier((sum_of_cores(own), messages))
    far = jnp.stack([message[:width] for message in messages]).astype(jnp.float32)

    flat = width % 128 == 0
    shape = (lambda n: (n, size * width)) if flat else (lambda n: (size, n, width))
    gram = pl.pallas_call(
        functools.partial(place_blocks, 1.0 / (rows * lax.axis_size("rows"))),
        out_shape=jax.ShapeDtypeStruct(shape(width), jnp.float32),
        in_specs=[SMEM] * 2 + [VMEM] * 4,
        out_specs=VMEM,
        compiler_params=params(16),
    )(where, (lax.axis_index("rows") & 1)[None], *sum_of_chips(own),
      *sum_of_chips(sum_of_cores(far)))
    rowwise = pl.pallas_call(
        functools.partial(filtered_rows, len(chunks)),
        out_shape=jax.ShapeDtypeStruct(shape(share), mine.dtype),
        in_specs=[SMEM] + [VMEM] * (1 + len(chunks) + len(messages)),
        out_specs=VMEM,
        compiler_params=params(16),
    )(where, mine, *chunks, *messages)
    if not flat:
        gram = gram.transpose(1, 0, 2).reshape(width, size * width)
        rowwise = rowwise.transpose(1, 0, 2).reshape(share, size * width)
    return rowwise, gram


def sum_of_cores(blocks):
    odd = lax.axis_index("rows") & 1
    half = blocks.shape[1] // 2
    keep = lax.dynamic_slice_in_dim(blocks, odd * half, half, 1)
    give = lax.dynamic_slice_in_dim(blocks, (1 - odd) * half, half, 1)
    return (keep + with_core(give)).astype(jnp.bfloat16)


def sum_of_chips(sent):
    size = lax.axis_size("rows")
    bit = 2
    while bit < size:
        got = lax.ppermute(sent, "rows", [(i, i ^ bit) for i in range(size)])
        total = sent.astype(jnp.float32) + got.astype(jnp.float32)
        sent = total.astype(jnp.bfloat16)
        bit *= 2
    return total, with_core(total)


def per_device(search_vectors, tile_values, block_columns):
    row_part = lax.axis_index("rows")
    col_parts = lax.axis_size("cols")
    count, tile, depth = tile_values.shape
    kt = block_columns.shape[1]
    assert REACH == count
    share = search_vectors.shape[0]
    width = search_vectors.shape[1] // col_parts
    rows = share * col_parts
    pieces = pl.pallas_call(
        split_columns,
        out_shape=jax.ShapeDtypeStruct((col_parts, share, width), search_vectors.dtype),
        in_specs=[VMEM],
        out_specs=VMEM,
        compiler_params=params(4),
    )(search_vectors)
    pieces, far_tiles = lax.optimization_barrier((pieces, tile_values))
    second = with_chip(far_tiles)
    columns = lax.all_to_all(pieces, "cols", split_axis=0, concat_axis=0, tiled=True)
    columns = columns.reshape(rows, width)

    size = HALO * tile
    odd = row_part & 1
    block_columns = block_columns.T
    inner = jnp.arange(count, dtype=jnp.int32)

    def offsets_of(columns, part):
        return jnp.clip(columns - (part * count + inner), -HALO, HALO)

    scratch = [
        pltpu.VMEM((HALO, kt + 1, tile, 2 * tile), jnp.bfloat16),
        pltpu.SMEM((HALO, 2 * HALO + 1), jnp.int32),
    ]
    bands, to_first, sent_columns = pl.pallas_call(
        own_bands,
        out_shape=(
            jax.ShapeDtypeStruct((count // HALO, size, SPAN * size), jnp.bfloat16),
            jax.ShapeDtypeStruct((TILES_REACH, tile, depth), jnp.bfloat16),
            jax.ShapeDtypeStruct((kt, count), jnp.int32),
        ),
        in_specs=[SMEM, SMEM, VMEM, VMEM, pl.BlockSpec(memory_space=pl.ANY)],
        out_specs=(VMEM,) * 3,
        scratch_shapes=scratch,
        compiler_params=params(16),
    )(odd[None], offsets_of(block_columns, row_part), block_columns, tile_values, pieces)
    first = with_core(to_first)
    at_first = with_core(sent_columns)
    at_second = with_chip(sent_columns)
    edges = pl.pallas_call(
        edge_bands,
        out_shape=jax.ShapeDtypeStruct(
            (2 * TILES_REACH // HALO, size, SPAN * size), jnp.bfloat16
        ),
        in_specs=[SMEM] * 3 + [VMEM] * 2,
        out_specs=VMEM,
        scratch_shapes=scratch,
        compiler_params=params(16),
    )(
        odd[None],
        offsets_of(at_first, row_part ^ 1),
        offsets_of(at_second, row_part - 1 + 2 * odd),
        first,
        second,
    )
    x_second = with_chip(columns)
    x_first = with_core(columns)

    window = [
        pltpu.VMEM((3 * rows, width), dtype)
        for dtype in (jnp.bfloat16, jnp.bfloat16, jnp.float32, jnp.float32)
    ]
    now, last, sent = pl.pallas_call(
        first_stage,
        out_shape=(
            jax.ShapeDtypeStruct((rows, width), jnp.float32),
            jax.ShapeDtypeStruct((rows + 2 * size, width), jnp.float32),
            jax.ShapeDtypeStruct((2 * rows - 2 * size, width), jnp.bfloat16),
        ),
        in_specs=[SMEM] + [VMEM] * 5,
        out_specs=(VMEM,) * 3,
        scratch_shapes=window,
        compiler_params=params(24),
    )(odd[None], bands, edges, x_first, columns, x_second)
    got_second = with_chip(sent)
    got_first = with_core(sent)
    filtered = pl.pallas_call(
        second_stage,
        out_shape=jax.ShapeDtypeStruct((rows, width), jnp.bfloat16),
        in_specs=[SMEM] + [VMEM] * 6,
        out_specs=VMEM,
        scratch_shapes=window,
        compiler_params=params(24),
    )(odd[None], bands, edges, now, last, got_first, got_second)

    return gram_and_rows(filtered)


def solution(mesh):
    return jax.shard_map(
        per_device,
        mesh=mesh,
        in_specs=(P(("rows", "cols"), None), P("rows", None, None), P("rows", None)),
        out_specs=(P(("rows", "cols"), None), P("cols", None)),
        check_vma=False,
    )
```

```python
import functools

import functools

import jax
import jax.numpy as jnp
from jax import lax
from jax.experimental import pallas as pl
from jax.experimental.pallas import tpu as pltpu
from jax.sharding import PartitionSpec as P

HALO = 4
DEGREE = 8
STAGE = 4
REACH = HALO * STAGE
TILES_REACH = REACH - HALO
SPAN = 3

shift_value = 0.1
half_width = 2.0

SMEM = pl.BlockSpec(memory_space=pltpu.SMEM)
VMEM = pl.BlockSpec(memory_space=pltpu.VMEM)


def params(mebibytes):
    return pltpu.CompilerParams(vmem_limit_bytes=mebibytes * 1024 * 1024)


def with_core(value):
    return lax.ppermute(value, "rows", [(i, i ^ 1) for i in range(lax.axis_size("rows"))])


def with_chip(value):
    odds = range(1, lax.axis_size("rows") - 1, 2)
    return lax.ppermute(value, "rows", [p for k in odds for p in ((k, k + 1), (k + 1, k))])


def place_group(offsets, ahead, tiles, start, bands, band, doubled, slot):
    kt = offsets.shape[0]
    tile = tiles.shape[1]
    blank = kt
    nothing = jnp.zeros((tile, tile), doubled.dtype)
    for i in range(HALO):
        values = tiles[start + i]
        for k in range(kt):
            one = values[:, k * tile:(k + 1) * tile]
            doubled[i, k] = jnp.concatenate([one, one], axis=1)
        for place in range(2 * HALO + 1):
            slot[i, place] = blank
        for k in range(kt):
            slot[i, offsets[k, ahead + start + i] + HALO] = k
    for i in range(HALO):
        rows = slice(i * tile, (i + 1) * tile)
        for pair in range(SPAN * HALO // 2):
            halves = []
            for side in range(2):
                place = 2 * pair + side - i
                if 0 <= place <= 2 * HALO:
                    both = doubled[i, slot[i, place]]
                    halves.append(both[:, side * tile:(side + 1) * tile])
                else:
                    halves.append(nothing)
            columns = slice(2 * pair * tile, 2 * (pair + 1) * tile)
            bands[band, rows, columns] = jnp.concatenate(halves, axis=1)


def clear(doubled):
    doubled[:, doubled.shape[1] - 1] = jnp.zeros(
        doubled.shape[:1] + doubled.shape[2:], doubled.dtype
    )


def split_columns(vectors, pieces):
    width = pieces.shape[2]
    for i in range(pieces.shape[0]):
        pieces[i] = vectors[:, i * width:(i + 1) * width]


def own_bands(odd, offsets, columns, tiles, _, bands, to_first, columns_out, doubled, slot):
    count = tiles.shape[0]
    sent = to_first.shape[0]
    to_first[...] = tiles[pl.ds((1 - odd[0]) * (count - sent), sent)]
    columns_out[...] = columns[...]
    clear(doubled)

    @pl.loop(0, count // HALO)
    def _(g):
        place_group(offsets, 0, tiles, g * HALO, bands, g, doubled, slot)


def edge_bands(odd, at_first, at_second, first, second, bands, doubled, slot):
    count = at_first.shape[1]
    edge = TILES_REACH // HALO
    clear(doubled)
    for offsets, tiles, behind in ((at_first, first, odd[0]), (at_second, second, 1 - odd[0])):
        begin = behind * (count - TILES_REACH)
        band = (1 - behind) * edge
        skipped = begin * (tiles.shape[0] // count)

        @pl.loop(0, edge)
        def _(g, offsets=offsets, tiles=tiles, begin=begin, band=band, skipped=skipped):
            place_group(offsets, begin - skipped, tiles, skipped + g * HALO, bands, band + g,
                        doubled, slot)


def run_steps(own, edges, w, y, degree):
    middle, size, span = own.shape
    edge = edges.shape[0] // 2
    bands = [edges.at[j] for j in range(edge)]
    bands += [own.at[j] for j in range(middle)]
    bands += [edges.at[edge + j] for j in range(edge)]
    groups = len(bands)
    cur, new = y
    src, dst = w
    for step in range(STAGE):
        for j in range(step, groups - step):
            start = j * size
            here = slice(start + size, start + 2 * size)
            product = dot(bands[j][...], src[start:start + span])
            value = product - shift_value * cur[here]
            value = value / half_width if degree + step == 0 else value - new[here]
            new[here] = value
            dst[here] = value.astype(jnp.bfloat16)
        cur, new = new, cur
        src, dst = dst, src
    return cur, new, src


def placed(behind, rows):
    return pl.multiple_of((1 - behind) * 2 * rows, rows)


def first_stage(odd, own, edges, x_first, x_own, x_second, now_out, last_out, sent_out,
                w0, w1, y0, y1):
    rows = x_own.shape[0]
    size = own.shape[1]
    starts = (placed(odd[0], rows), rows, placed(1 - odd[0], rows))
    for start, ref in zip(starts, (x_first, x_own, x_second)):
        w0[pl.ds(start, rows)] = ref[...]
        y0[pl.ds(start, rows)] = ref[...].astype(jnp.float32)
    cur, prev, rounded = run_steps(own, edges, (w0, w1), (y0, y1), 0)
    now_out[...] = cur[rows:2 * rows]
    last_out[...] = prev[rows - size:2 * rows + size]
    sent_out[:rows] = rounded[rows:2 * rows]
    sent_out[rows:] = prev[rows + size:2 * rows - size].astype(jnp.bfloat16)


def second_stage(odd, own, edges, now, last, got_first, got_second, out, w0, w1, y0, y1):
    rows = now.shape[0]
    size = own.shape[1]
    here = slice(rows, 2 * rows)
    w0[here] = now[...].astype(jnp.bfloat16)
    y0[here] = now[...]
    y1[rows - size:2 * rows + size] = last[...]
    for got, behind in ((got_first, odd[0]), (got_second, 1 - odd[0])):
        start = placed(behind, rows)
        w0[pl.ds(start, rows)] = got[:rows]
        y0[pl.ds(start, rows)] = got[:rows].astype(jnp.float32)
        y1[pl.ds(pl.multiple_of(start + size, size), rows - 2 * size)] = (
            got[rows:].astype(jnp.float32)
        )
    _, _, rounded = run_steps(own, edges, (w0, w1), (y0, y1), STAGE)
    out[...] = rounded[here]


def dot(a, b):
    return jnp.dot(a, b, preferred_element_type=jnp.float32)


def columns_at(ref, group, width):
    if len(ref.shape) == 2:
        return slice(None), pl.ds(pl.multiple_of(group * width, width), width)
    return (group,)


def early_gram(mine, *refs):
    *blocks, partial, lefts = refs
    left = mine[...].T
    lefts[0] = left
    for t, ref in enumerate((mine, *blocks)):
        block = ref[...]
        if t:
            lefts[t] = block.T
        partial[t] = dot(left, block)


def far_messages(where, lefts, back, front, *messages):
    width = lefts.shape[1]
    share = messages[0].shape[0] - width
    reach = lefts.shape[0] // 2 + 1
    far_back, far_front = back[...], front[...]
    made = []
    for t in range(1, reach):
        made.append((dot(lefts[2 * t], far_back), back, where[2 * t]))
        made.append((dot(lefts[2 * t - 1], far_front), front, where[2 * t - 1]))
    made.append((dot(far_back.T, far_front), front, where[2 * reach - 1]))
    for message, (block, source, device) in zip(messages, made):
        message[:width] = block.astype(message.dtype)
        message[width:] = source[pl.ds(pl.multiple_of(device * share, share), share)]


def own_blocks(lefts, early, back, front, _, partial):
    held = early.shape[0]
    partial[:held] = early[...]
    partial[held] = dot(lefts[0], back[...])
    partial[held + 1] = dot(lefts[0], front[...])


def place_blocks(scale, where, odd, *refs):
    own, own_other, far, far_other, gram = refs
    half, width = own.shape[1:]
    first = own.shape[0]
    for side, (near, distant) in enumerate(((own, far), (own_other, far_other))):
        rows = pl.ds(pl.multiple_of((odd[0] ^ side) * half, half), half)
        for t in range(first + far.shape[0]):
            block = near[t] if t < first else distant[t - first]
            if len(gram.shape) == 2:
                start = pl.multiple_of(where[t] * width, width)
                gram[rows, pl.ds(start, width)] = block * scale
            else:
                gram[where[t], rows] = block * scale


def filtered_rows(number, where, mine, *refs):
    blocks, messages, rowwise = (mine,) + refs[:number], refs[number:-1], refs[-1]
    width = mine.shape[1]
    share = rowwise.shape[-2]
    start = pl.multiple_of(where[0] * share, share)
    for t, block in enumerate(blocks):
        rowwise[columns_at(rowwise, where[t], width)] = block[pl.ds(start, share)]
    for t, message in enumerate(messages):
        rowwise[columns_at(rowwise, where[1 + number + t], width)] = message[width:]


def ring_of(size):
    return list(range(0, size, 2)) + list(range(size - 1, 0, -2))


def gram_and_rows(mine):
    size = lax.axis_size("cols")
    device = lax.axis_index("cols")
    assert size % 4 == 0
    reach = size // 4
    order = ring_of(size)
    rows, width = mine.shape
    share = rows // size

    def move(value, by):
        return lax.ppermute(
            value, "cols", [(order[i], order[(i + by) % size]) for i in range(size)]
        )

    fetched = {by: move(mine, by) for t in range(reach, 0, -1) for by in (t, -t)}
    blocks, steps = [], [0]
    for t in range(1, reach + 1):
        blocks += [fetched[t], fetched[-t]]
        steps += [-t, t]
    sends = [by for t in range(1, reach) for by in (t, -t)] + [-reach]
    steps += [-(by + reach) if by > 0 else reach - by for by in sends]

    place = jnp.where(device % 2 == 0, device // 2, size - 1 - device // 2)
    where = (place + jnp.array(steps, jnp.int32)) % size
    where = jnp.where(where < size // 2, 2 * where, 2 * (size - 1 - where) + 1)

    held = 2 * reach - 1
    early, lefts = pl.pallas_call(
        early_gram,
        out_shape=(
            jax.ShapeDtypeStruct((held, width, width), jnp.float32),
            jax.ShapeDtypeStruct((held, width, rows), mine.dtype),
        ),
        in_specs=[VMEM] * held,
        out_specs=(VMEM, VMEM),
        compiler_params=params(16),
    )(mine, *blocks[:-2])
    message = jax.ShapeDtypeStruct((width + share, width), mine.dtype)
    messages = pl.pallas_call(
        far_messages,
        out_shape=(message,) * len(sends),
        in_specs=[SMEM] + [VMEM] * 3,
        out_specs=(VMEM,) * len(sends),
        compiler_params=params(16),
    )(where, lefts, *blocks[-2:])
    own = pl.pallas_call(
        own_blocks,
        out_shape=jax.ShapeDtypeStruct((held + 2, width, width), jnp.float32),
        in_specs=[VMEM] * 4 + [pl.BlockSpec(memory_space=pl.ANY)],
        out_specs=VMEM,
        compiler_params=params(16),
    )(lefts, early, *blocks[-2:], messages[-1])
    messages = [move(value, by) for value, by in zip(messages, sends)]
    own, messages = lax.optimization_barrier((sum_of_cores(own), messages))
    far = jnp.stack([message[:width] for message in messages]).astype(jnp.float32)

    flat = width % 128 == 0
    shape = (lambda n: (n, size * width)) if flat else (lambda n: (size, n, width))
    gram = pl.pallas_call(
        functools.partial(place_blocks, 1.0 / (rows * lax.axis_size("rows"))),
        out_shape=jax.ShapeDtypeStruct(shape(width), jnp.float32),
        in_specs=[SMEM] * 2 + [VMEM] * 4,
        out_specs=VMEM,
        compiler_params=params(16),
    )(where, (lax.axis_index("rows") & 1)[None], *sum_of_chips(own),
      *sum_of_chips(sum_of_cores(far)))
    rowwise = pl.pallas_call(
        functools.partial(filtered_rows, len(blocks)),
        out_shape=jax.ShapeDtypeStruct(shape(share), mine.dtype),
        in_specs=[SMEM] + [VMEM] * (1 + len(blocks) + len(messages)),
        out_specs=VMEM,
        compiler_params=params(16),
    )(where, mine, *blocks, *messages)
    if not flat:
        gram = gram.transpose(1, 0, 2).reshape(width, size * width)
        rowwise = rowwise.transpose(1, 0, 2).reshape(share, size * width)
    return rowwise, gram


def sum_of_cores(blocks):
    odd = lax.axis_index("rows") & 1
    half = blocks.shape[1] // 2
    keep = lax.dynamic_slice_in_dim(blocks, odd * half, half, 1)
    give = lax.dynamic_slice_in_dim(blocks, (1 - odd) * half, half, 1)
    return (keep + with_core(give)).astype(jnp.bfloat16)


def sum_of_chips(sent):
    size = lax.axis_size("rows")
    bit = 2
    while bit < size:
        got = lax.ppermute(sent, "rows", [(i, i ^ bit) for i in range(size)])
        total = sent.astype(jnp.float32) + got.astype(jnp.float32)
        sent = total.astype(jnp.bfloat16)
        bit *= 2
    return total, with_core(total)


def per_device(search_vectors, tile_values, block_columns):
    row_part = lax.axis_index("rows")
    col_parts = lax.axis_size("cols")
    count, tile, depth = tile_values.shape
    kt = block_columns.shape[1]
    assert REACH == count
    share = search_vectors.shape[0]
    width = search_vectors.shape[1] // col_parts
    rows = share * col_parts
    second = with_chip(tile_values)
    pieces = pl.pallas_call(
        split_columns,
        out_shape=jax.ShapeDtypeStruct((col_parts, share, width), search_vectors.dtype),
        in_specs=[VMEM],
        out_specs=VMEM,
        compiler_params=params(4),
    )(search_vectors)
    columns = lax.all_to_all(pieces, "cols", split_axis=0, concat_axis=0, tiled=True)
    columns = columns.reshape(rows, width)

    size = HALO * tile
    odd = row_part & 1
    block_columns = block_columns.T
    inner = jnp.arange(count, dtype=jnp.int32)

    def offsets_of(columns, part):
        return jnp.clip(columns - (part * count + inner), -HALO, HALO)

    scratch = [
        pltpu.VMEM((HALO, kt + 1, tile, 2 * tile), jnp.bfloat16),
        pltpu.SMEM((HALO, 2 * HALO + 1), jnp.int32),
    ]
    bands, to_first, sent_columns = pl.pallas_call(
        own_bands,
        out_shape=(
            jax.ShapeDtypeStruct((count // HALO, size, SPAN * size), jnp.bfloat16),
            jax.ShapeDtypeStruct((TILES_REACH, tile, depth), jnp.bfloat16),
            jax.ShapeDtypeStruct((kt, count), jnp.int32),
        ),
        in_specs=[SMEM, SMEM, VMEM, VMEM, pl.BlockSpec(memory_space=pl.ANY)],
        out_specs=(VMEM,) * 3,
        scratch_shapes=scratch,
        compiler_params=params(16),
    )(odd[None], offsets_of(block_columns, row_part), block_columns, tile_values, pieces)
    first = with_core(to_first)
    at_first = with_core(sent_columns)
    at_second = with_chip(sent_columns)
    edges = pl.pallas_call(
        edge_bands,
        out_shape=jax.ShapeDtypeStruct(
            (2 * TILES_REACH // HALO, size, SPAN * size), jnp.bfloat16
        ),
        in_specs=[SMEM] * 3 + [VMEM] * 2,
        out_specs=VMEM,
        scratch_shapes=scratch,
        compiler_params=params(16),
    )(
        odd[None],
        offsets_of(at_first, row_part ^ 1),
        offsets_of(at_second, row_part - 1 + 2 * odd),
        first,
        second,
    )
    x_second = with_chip(columns)
    x_first = with_core(columns)

    window = [
        pltpu.VMEM((3 * rows, width), dtype)
        for dtype in (jnp.bfloat16, jnp.bfloat16, jnp.float32, jnp.float32)
    ]
    now, last, sent = pl.pallas_call(
        first_stage,
        out_shape=(
            jax.ShapeDtypeStruct((rows, width), jnp.float32),
            jax.ShapeDtypeStruct((rows + 2 * size, width), jnp.float32),
            jax.ShapeDtypeStruct((2 * rows - 2 * size, width), jnp.bfloat16),
        ),
        in_specs=[SMEM] + [VMEM] * 5,
        out_specs=(VMEM,) * 3,
        scratch_shapes=window,
        compiler_params=params(24),
    )(odd[None], bands, edges, x_first, columns, x_second)
    got_second = with_chip(sent)
    got_first = with_core(sent)
    filtered = pl.pallas_call(
        second_stage,
        out_shape=jax.ShapeDtypeStruct((rows, width), jnp.bfloat16),
        in_specs=[SMEM] + [VMEM] * 6,
        out_specs=VMEM,
        scratch_shapes=window,
        compiler_params=params(24),
    )(odd[None], bands, edges, now, last, got_first, got_second)

    return gram_and_rows(filtered)


def solution(mesh):
    return jax.shard_map(
        per_device,
        mesh=mesh,
        in_specs=(P(("rows", "cols"), None), P("rows", None, None), P("rows", None)),
        out_specs=(P(("rows", "cols"), None), P("cols", None)),
        check_vma=False,
    )
```

```python
import functools

import functools

import jax
import jax.numpy as jnp
from jax import lax
from jax.experimental import pallas as pl
from jax.experimental.pallas import tpu as pltpu
from jax.sharding import PartitionSpec as P

HALO = 4
DEGREE = 8
STAGE = 4
REACH = HALO * STAGE
TILES_REACH = REACH - HALO
SPAN = 3

shift_value = 0.1
half_width = 2.0

SMEM = pl.BlockSpec(memory_space=pltpu.SMEM)
VMEM = pl.BlockSpec(memory_space=pltpu.VMEM)
ANY = pl.BlockSpec(memory_space=pl.ANY)


def params(mebibytes):
    return pltpu.CompilerParams(vmem_limit_bytes=mebibytes * 1024 * 1024)


def with_core(value):
    return lax.ppermute(value, "rows", [(i, i ^ 1) for i in range(lax.axis_size("rows"))])


def with_chip(value):
    odds = range(1, lax.axis_size("rows") - 1, 2)
    return lax.ppermute(value, "rows", [p for k in odds for p in ((k, k + 1), (k + 1, k))])


def place_group(offsets, ahead, tiles, start, bands, band, doubled, slot):
    kt = offsets.shape[0]
    tile = tiles.shape[1]
    blank = kt
    nothing = jnp.zeros((tile, tile), doubled.dtype)
    for i in range(HALO):
        values = tiles[start + i]
        for k in range(kt):
            one = values[:, k * tile:(k + 1) * tile]
            doubled[i, k] = jnp.concatenate([one, one], axis=1)
        for place in range(2 * HALO + 1):
            slot[i, place] = blank
        for k in range(kt):
            slot[i, offsets[k, ahead + start + i] + HALO] = k
    for i in range(HALO):
        rows = slice(i * tile, (i + 1) * tile)
        for pair in range(SPAN * HALO // 2):
            halves = []
            for side in range(2):
                place = 2 * pair + side - i
                if 0 <= place <= 2 * HALO:
                    both = doubled[i, slot[i, place]]
                    halves.append(both[:, side * tile:(side + 1) * tile])
                else:
                    halves.append(nothing)
            columns = slice(2 * pair * tile, 2 * (pair + 1) * tile)
            bands[band, rows, columns] = jnp.concatenate(halves, axis=1)


def clear(doubled):
    doubled[:, doubled.shape[1] - 1] = jnp.zeros(
        doubled.shape[:1] + doubled.shape[2:], doubled.dtype
    )


def split_columns(vectors, pieces):
    width = pieces.shape[2]
    for i in range(pieces.shape[0]):
        pieces[i] = vectors[:, i * width:(i + 1) * width]


def copy_columns(vectors, pieces, done):
    width = pieces.shape[2]
    copies = [
        pltpu.make_async_copy(
            vectors.at[:, i * width:(i + 1) * width], pieces.at[i], done.at[i]
        )
        for i in range(pieces.shape[0])
    ]
    for copy in copies:
        copy.start()
    for copy in copies:
        copy.wait()


def own_bands(odd, offsets, columns, tiles, _, bands, to_first, columns_out, doubled, slot):
    count = tiles.shape[0]
    sent = to_first.shape[0]
    to_first[...] = tiles[pl.ds((1 - odd[0]) * (count - sent), sent)]
    columns_out[...] = columns[...]
    clear(doubled)

    @pl.loop(0, count // HALO)
    def _(g):
        place_group(offsets, 0, tiles, g * HALO, bands, g, doubled, slot)


def edge_bands(odd, at_first, at_second, first, second, bands, doubled, slot):
    count = at_first.shape[1]
    edge = TILES_REACH // HALO
    clear(doubled)
    for offsets, tiles, behind in ((at_first, first, odd[0]), (at_second, second, 1 - odd[0])):
        begin = behind * (count - TILES_REACH)
        band = (1 - behind) * edge
        skipped = begin * (tiles.shape[0] // count)

        @pl.loop(0, edge)
        def _(g, offsets=offsets, tiles=tiles, begin=begin, band=band, skipped=skipped):
            place_group(offsets, begin - skipped, tiles, skipped + g * HALO, bands, band + g,
                        doubled, slot)


def run_steps(own, edges, w, y, degree):
    middle, size, span = own.shape
    edge = edges.shape[0] // 2
    bands = [edges.at[j] for j in range(edge)]
    bands += [own.at[j] for j in range(middle)]
    bands += [edges.at[edge + j] for j in range(edge)]
    groups = len(bands)
    cur, new = y
    src, dst = w
    for step in range(STAGE):
        for j in range(step, groups - step):
            start = j * size
            here = slice(start + size, start + 2 * size)
            product = dot(bands[j][...], src[start:start + span])
            value = product - shift_value * cur[here]
            value = value / half_width if degree + step == 0 else value - new[here]
            new[here] = value
            dst[here] = value.astype(jnp.bfloat16)
        cur, new = new, cur
        src, dst = dst, src
    return cur, new, src


def placed(behind, rows):
    return pl.multiple_of((1 - behind) * 2 * rows, rows)


def first_stage(odd, own, edges, x_first, x_own, x_second, now_out, last_out, sent_out,
                w0, w1, y0, y1):
    rows = x_own.shape[0]
    size = own.shape[1]
    starts = (placed(odd[0], rows), rows, placed(1 - odd[0], rows))
    for start, ref in zip(starts, (x_first, x_own, x_second)):
        w0[pl.ds(start, rows)] = ref[...]
        y0[pl.ds(start, rows)] = ref[...].astype(jnp.float32)
    cur, prev, rounded = run_steps(own, edges, (w0, w1), (y0, y1), 0)
    now_out[...] = cur[rows:2 * rows]
    last_out[...] = prev[rows - size:2 * rows + size]
    sent_out[:rows] = rounded[rows:2 * rows]
    sent_out[rows:] = prev[rows + size:2 * rows - size].astype(jnp.bfloat16)


def second_stage(odd, own, edges, now, last, got_first, got_second, out, w0, w1, y0, y1):
    rows = now.shape[0]
    size = own.shape[1]
    here = slice(rows, 2 * rows)
    w0[here] = now[...].astype(jnp.bfloat16)
    y0[here] = now[...]
    y1[rows - size:2 * rows + size] = last[...]
    for got, behind in ((got_first, odd[0]), (got_second, 1 - odd[0])):
        start = placed(behind, rows)
        w0[pl.ds(start, rows)] = got[:rows]
        y0[pl.ds(start, rows)] = got[:rows].astype(jnp.float32)
        y1[pl.ds(pl.multiple_of(start + size, size), rows - 2 * size)] = (
            got[rows:].astype(jnp.float32)
        )
    _, _, rounded = run_steps(own, edges, (w0, w1), (y0, y1), STAGE)
    out[...] = rounded[here]


def dot(a, b):
    return jnp.dot(a, b, preferred_element_type=jnp.float32)


def columns_at(ref, group, width):
    if len(ref.shape) == 2:
        return slice(None), pl.ds(pl.multiple_of(group * width, width), width)
    return (group,)


def early_gram(mine, *refs):
    *blocks, partial, lefts = refs
    left = mine[...].T
    lefts[0] = left
    for t, ref in enumerate((mine, *blocks)):
        block = ref[...]
        if t:
            lefts[t] = block.T
        partial[t] = dot(left, block)


def far_messages(where, lefts, back, front, *messages):
    width = lefts.shape[1]
    share = messages[0].shape[0] - width
    reach = lefts.shape[0] // 2 + 1
    far_back, far_front = back[...], front[...]
    made = []
    for t in range(1, reach):
        made.append((dot(lefts[2 * t], far_back), back, where[2 * t]))
        made.append((dot(lefts[2 * t - 1], far_front), front, where[2 * t - 1]))
    made.append((dot(far_back.T, far_front), front, where[2 * reach - 1]))
    for message, (block, source, device) in zip(messages, made):
        message[:width] = block.astype(message.dtype)
        message[width:] = source[pl.ds(pl.multiple_of(device * share, share), share)]


def own_blocks(lefts, early, back, front, _, partial):
    held = early.shape[0]
    partial[:held] = early[...]
    partial[held] = dot(lefts[0], back[...])
    partial[held + 1] = dot(lefts[0], front[...])


def place_blocks(scale, where, odd, *refs):
    own, own_other, far, far_other, gram = refs
    half, width = own.shape[1:]
    first = own.shape[0]
    for side, (near, distant) in enumerate(((own, far), (own_other, far_other))):
        rows = pl.ds(pl.multiple_of((odd[0] ^ side) * half, half), half)
        for t in range(first + far.shape[0]):
            block = near[t] if t < first else distant[t - first]
            if len(gram.shape) == 2:
                start = pl.multiple_of(where[t] * width, width)
                gram[rows, pl.ds(start, width)] = block * scale
            else:
                gram[where[t], rows] = block * scale


def filtered_rows(number, where, mine, *refs):
    blocks, messages, rowwise = (mine,) + refs[:number], refs[number:-1], refs[-1]
    width = mine.shape[1]
    share = rowwise.shape[-2]
    start = pl.multiple_of(where[0] * share, share)
    for t, block in enumerate(blocks):
        rowwise[columns_at(rowwise, where[t], width)] = block[pl.ds(start, share)]
    for t, message in enumerate(messages):
        rowwise[columns_at(rowwise, where[1 + number + t], width)] = message[width:]


def ring_of(size):
    return list(range(0, size, 2)) + list(range(size - 1, 0, -2))


def gram_and_rows(mine):
    size = lax.axis_size("cols")
    device = lax.axis_index("cols")
    assert size % 4 == 0
    reach = size // 4
    order = ring_of(size)
    rows, width = mine.shape
    share = rows // size

    def move(value, by):
        return lax.ppermute(
            value, "cols", [(order[i], order[(i + by) % size]) for i in range(size)]
        )

    fetched = {by: move(mine, by) for t in range(reach, 0, -1) for by in (t, -t)}
    blocks, steps = [], [0]
    for t in range(1, reach + 1):
        blocks += [fetched[t], fetched[-t]]
        steps += [-t, t]
    sends = [by for t in range(1, reach) for by in (t, -t)] + [-reach]
    steps += [-(by + reach) if by > 0 else reach - by for by in sends]

    place = jnp.where(device % 2 == 0, device // 2, size - 1 - device // 2)
    where = (place + jnp.array(steps, jnp.int32)) % size
    where = jnp.where(where < size // 2, 2 * where, 2 * (size - 1 - where) + 1)

    held = 2 * reach - 1
    early, lefts = pl.pallas_call(
        early_gram,
        out_shape=(
            jax.ShapeDtypeStruct((held, width, width), jnp.float32),
            jax.ShapeDtypeStruct((held, width, rows), mine.dtype),
        ),
        in_specs=[VMEM] * held,
        out_specs=(VMEM, VMEM),
        compiler_params=params(16),
    )(mine, *blocks[:-2])
    message = jax.ShapeDtypeStruct((width + share, width), mine.dtype)
    messages = pl.pallas_call(
        far_messages,
        out_shape=(message,) * len(sends),
        in_specs=[SMEM] + [VMEM] * 3,
        out_specs=(VMEM,) * len(sends),
        compiler_params=params(16),
    )(where, lefts, *blocks[-2:])
    own = pl.pallas_call(
        own_blocks,
        out_shape=jax.ShapeDtypeStruct((held + 2, width, width), jnp.float32),
        in_specs=[VMEM] * 4 + [ANY],
        out_specs=VMEM,
        compiler_params=params(16),
    )(lefts, early, *blocks[-2:], messages[-1])
    messages = [move(value, by) for value, by in zip(messages, sends)]
    own, messages = lax.optimization_barrier((sum_of_cores(own), messages))
    far = jnp.stack([message[:width] for message in messages]).astype(jnp.float32)

    flat = width % 128 == 0
    shape = (lambda n: (n, size * width)) if flat else (lambda n: (size, n, width))
    far = sum_of_cores(far)
    rowwise = pl.pallas_call(
        functools.partial(filtered_rows, len(blocks)),
        out_shape=jax.ShapeDtypeStruct(shape(share), mine.dtype),
        in_specs=[SMEM] + [VMEM] * (1 + len(blocks) + len(messages)),
        out_specs=VMEM,
        compiler_params=params(16),
    )(where, mine, *blocks, *messages)
    own = sum_of_chips(own)
    far = sum_of_chips(far)
    gram = pl.pallas_call(
        functools.partial(place_blocks, 1.0 / (rows * lax.axis_size("rows"))),
        out_shape=jax.ShapeDtypeStruct(shape(width), jnp.float32),
        in_specs=[SMEM] * 2 + [VMEM] * 4,
        out_specs=VMEM,
        compiler_params=params(16),
    )(where, (lax.axis_index("rows") & 1)[None], own, with_core(own), far, with_core(far))
    if not flat:
        gram = gram.transpose(1, 0, 2).reshape(width, size * width)
        rowwise = rowwise.transpose(1, 0, 2).reshape(share, size * width)
    return rowwise, gram


def sum_of_cores(blocks):
    odd = lax.axis_index("rows") & 1
    half = blocks.shape[1] // 2
    keep = lax.dynamic_slice_in_dim(blocks, odd * half, half, 1)
    give = lax.dynamic_slice_in_dim(blocks, (1 - odd) * half, half, 1)
    return (keep + with_core(give)).astype(jnp.bfloat16)


def sum_of_chips(sent):
    size = lax.axis_size("rows")
    total = sent.astype(jnp.float32)
    bit = 2
    while bit < size:
        got = lax.ppermute(sent, "rows", [(i, i ^ bit) for i in range(size)])
        total = sent.astype(jnp.float32) + got.astype(jnp.float32)
        sent = total.astype(jnp.bfloat16)
        bit *= 2
    return total


def per_device(search_vectors, tile_values, block_columns):
    row_part = lax.axis_index("rows")
    col_parts = lax.axis_size("cols")
    count, tile, depth = tile_values.shape
    kt = block_columns.shape[1]
    assert REACH == count
    share = search_vectors.shape[0]
    width = search_vectors.shape[1] // col_parts
    rows = share * col_parts
    second = with_chip(tile_values)
    lanes = width % 128 == 0
    pieces = pl.pallas_call(
        copy_columns if lanes else split_columns,
        out_shape=jax.ShapeDtypeStruct((col_parts, share, width), search_vectors.dtype),
        in_specs=[pl.BlockSpec(memory_space=pltpu.HBM) if lanes else VMEM],
        out_specs=pl.BlockSpec(memory_space=pltpu.HBM) if lanes else VMEM,
        scratch_shapes=[pltpu.SemaphoreType.DMA((col_parts,))] if lanes else [],
        compiler_params=params(4),
    )(search_vectors)
    columns = lax.all_to_all(pieces, "cols", split_axis=0, concat_axis=0, tiled=True)
    columns = columns.reshape(rows, width)

    size = HALO * tile
    odd = row_part & 1
    block_columns = block_columns.T
    inner = jnp.arange(count, dtype=jnp.int32)

    def offsets_of(columns, part):
        return jnp.clip(columns - (part * count + inner), -HALO, HALO)

    scratch = [
        pltpu.VMEM((HALO, kt + 1, tile, 2 * tile), jnp.bfloat16),
        pltpu.SMEM((HALO, 2 * HALO + 1), jnp.int32),
    ]
    bands, to_first, sent_columns = pl.pallas_call(
        own_bands,
        out_shape=(
            jax.ShapeDtypeStruct((count // HALO, size, SPAN * size), jnp.bfloat16),
            jax.ShapeDtypeStruct((TILES_REACH, tile, depth), jnp.bfloat16),
            jax.ShapeDtypeStruct((kt, count), jnp.int32),
        ),
        in_specs=[SMEM, SMEM, VMEM, VMEM, ANY],
        out_specs=(VMEM,) * 3,
        scratch_shapes=scratch,
        compiler_params=params(16),
    )(odd[None], offsets_of(block_columns, row_part), block_columns, tile_values, pieces)
    first = with_core(to_first)
    at_first = with_core(sent_columns)
    at_second = with_chip(sent_columns)
    edges = pl.pallas_call(
        edge_bands,
        out_shape=jax.ShapeDtypeStruct(
            (2 * TILES_REACH // HALO, size, SPAN * size), jnp.bfloat16
        ),
        in_specs=[SMEM] * 3 + [VMEM] * 2,
        out_specs=VMEM,
        scratch_shapes=scratch,
        compiler_params=params(16),
    )(
        odd[None],
        offsets_of(at_first, row_part ^ 1),
        offsets_of(at_second, row_part - 1 + 2 * odd),
        first,
        second,
    )
    x_second = with_chip(columns)
    x_first = with_core(columns)

    window = [
        pltpu.VMEM((3 * rows, width), dtype)
        for dtype in (jnp.bfloat16, jnp.bfloat16, jnp.float32, jnp.float32)
    ]
    now, last, sent = pl.pallas_call(
        first_stage,
        out_shape=(
            jax.ShapeDtypeStruct((rows, width), jnp.float32),
            jax.ShapeDtypeStruct((rows + 2 * size, width), jnp.float32),
            jax.ShapeDtypeStruct((2 * rows - 2 * size, width), jnp.bfloat16),
        ),
        in_specs=[SMEM] + [VMEM] * 5,
        out_specs=(VMEM,) * 3,
        scratch_shapes=window,
        compiler_params=params(24),
    )(odd[None], bands, edges, x_first, columns, x_second)
    got_second = with_chip(sent)
    got_first = with_core(sent)
    filtered = pl.pallas_call(
        second_stage,
        out_shape=jax.ShapeDtypeStruct((rows, width), jnp.bfloat16),
        in_specs=[SMEM] + [VMEM] * 6,
        out_specs=VMEM,
        scratch_shapes=window,
        compiler_params=params(24),
    )(odd[None], bands, edges, now, last, got_first, got_second)

    return gram_and_rows(filtered)


def solution(mesh):
    return jax.shard_map(
        per_device,
        mesh=mesh,
        in_specs=(P(("rows", "cols"), None), P("rows", None, None), P("rows", None)),
        out_specs=(P(("rows", "cols"), None), P("cols", None)),
        check_vma=False,
    )
```

```python
import functools

import functools

import jax
import jax.numpy as jnp
from jax import lax
from jax.experimental import pallas as pl
from jax.experimental.pallas import tpu as pltpu
from jax.sharding import PartitionSpec as P

HALO = 4
DEGREE = 8
STAGE = 4
REACH = HALO * STAGE
TILES_REACH = REACH - HALO
SPAN = 3

shift_value = 0.1
half_width = 2.0

SMEM = pl.BlockSpec(memory_space=pltpu.SMEM)
VMEM = pl.BlockSpec(memory_space=pltpu.VMEM)
ANY = pl.BlockSpec(memory_space=pl.ANY)


def params(mebibytes):
    return pltpu.CompilerParams(vmem_limit_bytes=mebibytes * 1024 * 1024)


def with_core(value):
    return lax.ppermute(value, "rows", [(i, i ^ 1) for i in range(lax.axis_size("rows"))])


def with_chip(value):
    odds = range(1, lax.axis_size("rows") - 1, 2)
    return lax.ppermute(value, "rows", [p for k in odds for p in ((k, k + 1), (k + 1, k))])


def place_group(offsets, ahead, tiles, start, bands, band, doubled, slot):
    kt = offsets.shape[0]
    tile = tiles.shape[1]
    blank = kt
    nothing = jnp.zeros((tile, tile), doubled.dtype)
    for i in range(HALO):
        values = tiles[start + i]
        for k in range(kt):
            one = values[:, k * tile:(k + 1) * tile]
            doubled[i, k] = jnp.concatenate([one, one], axis=1)
        for place in range(2 * HALO + 1):
            slot[i, place] = blank
        for k in range(kt):
            slot[i, offsets[k, ahead + start + i] + HALO] = k
    for i in range(HALO):
        rows = slice(i * tile, (i + 1) * tile)
        for pair in range(SPAN * HALO // 2):
            halves = []
            for side in range(2):
                place = 2 * pair + side - i
                if 0 <= place <= 2 * HALO:
                    both = doubled[i, slot[i, place]]
                    halves.append(both[:, side * tile:(side + 1) * tile])
                else:
                    halves.append(nothing)
            columns = slice(2 * pair * tile, 2 * (pair + 1) * tile)
            bands[band, rows, columns] = jnp.concatenate(halves, axis=1)


def clear(doubled):
    doubled[:, doubled.shape[1] - 1] = jnp.zeros(
        doubled.shape[:1] + doubled.shape[2:], doubled.dtype
    )


def split_columns(vectors, pieces):
    width = pieces.shape[2]
    for i in range(pieces.shape[0]):
        pieces[i] = vectors[:, i * width:(i + 1) * width]


def copy_columns(vectors, pieces, done):
    width = pieces.shape[2]
    copies = [
        pltpu.make_async_copy(
            vectors.at[:, i * width:(i + 1) * width], pieces.at[i], done.at[i]
        )
        for i in range(pieces.shape[0])
    ]
    for copy in copies:
        copy.start()
    for copy in copies:
        copy.wait()


def own_bands(odd, offsets, columns, tiles, _, bands, to_first, columns_out, doubled, slot):
    count = tiles.shape[0]
    sent = to_first.shape[0]
    to_first[...] = tiles[pl.ds((1 - odd[0]) * (count - sent), sent)]
    columns_out[...] = columns[...]
    clear(doubled)

    @pl.loop(0, count // HALO)
    def _(g):
        place_group(offsets, 0, tiles, g * HALO, bands, g, doubled, slot)


def edge_bands(odd, at_first, at_second, first, second, bands, doubled, slot):
    count = at_first.shape[1]
    edge = TILES_REACH // HALO
    clear(doubled)
    for offsets, tiles, behind in ((at_first, first, odd[0]), (at_second, second, 1 - odd[0])):
        begin = behind * (count - TILES_REACH)
        band = (1 - behind) * edge
        skipped = begin * (tiles.shape[0] // count)

        @pl.loop(0, edge)
        def _(g, offsets=offsets, tiles=tiles, begin=begin, band=band, skipped=skipped):
            place_group(offsets, begin - skipped, tiles, skipped + g * HALO, bands, band + g,
                        doubled, slot)


def run_steps(own, edges, w, y, degree):
    middle, size, span = own.shape
    edge = edges.shape[0] // 2
    bands = [edges.at[j] for j in range(edge)]
    bands += [own.at[j] for j in range(middle)]
    bands += [edges.at[edge + j] for j in range(edge)]
    groups = len(bands)
    cur, new = y
    src, dst = w
    for step in range(STAGE):
        for j in range(step, groups - step):
            start = j * size
            here = slice(start + size, start + 2 * size)
            product = dot(bands[j][...], src[start:start + span])
            value = product - shift_value * cur[here]
            value = value / half_width if degree + step == 0 else value - new[here]
            new[here] = value
            dst[here] = value.astype(jnp.bfloat16)
        cur, new = new, cur
        src, dst = dst, src
    return cur, new, src


def placed(behind, rows):
    return pl.multiple_of((1 - behind) * 2 * rows, rows)


def first_stage(odd, own, edges, x_first, x_own, x_second, now_out, last_out, sent_out,
                w0, w1, y0, y1):
    rows = x_own.shape[0]
    size = own.shape[1]
    starts = (placed(odd[0], rows), rows, placed(1 - odd[0], rows))
    for start, ref in zip(starts, (x_first, x_own, x_second)):
        w0[pl.ds(start, rows)] = ref[...]
        y0[pl.ds(start, rows)] = ref[...].astype(jnp.float32)
    cur, prev, rounded = run_steps(own, edges, (w0, w1), (y0, y1), 0)
    now_out[...] = cur[rows:2 * rows]
    last_out[...] = prev[rows - size:2 * rows + size]
    sent_out[:rows] = rounded[rows:2 * rows]
    sent_out[rows:] = prev[rows + size:2 * rows - size].astype(jnp.bfloat16)


def second_stage(odd, own, edges, now, last, got_first, got_second, out, w0, w1, y0, y1):
    rows = now.shape[0]
    size = own.shape[1]
    here = slice(rows, 2 * rows)
    w0[here] = now[...].astype(jnp.bfloat16)
    y0[here] = now[...]
    y1[rows - size:2 * rows + size] = last[...]
    for got, behind in ((got_first, odd[0]), (got_second, 1 - odd[0])):
        start = placed(behind, rows)
        w0[pl.ds(start, rows)] = got[:rows]
        y0[pl.ds(start, rows)] = got[:rows].astype(jnp.float32)
        y1[pl.ds(pl.multiple_of(start + size, size), rows - 2 * size)] = (
            got[rows:].astype(jnp.float32)
        )
    _, _, rounded = run_steps(own, edges, (w0, w1), (y0, y1), STAGE)
    out[...] = rounded[here]


def dot(a, b):
    return jnp.dot(a, b, preferred_element_type=jnp.float32)


def columns_at(ref, group, width):
    if len(ref.shape) == 2:
        return slice(None), pl.ds(pl.multiple_of(group * width, width), width)
    return (group,)


def early_gram(where, mine, back, front, partial, lefts, message):
    width = lefts.shape[1]
    share = message.shape[0] - width
    far_front = front[...]
    left = mine[...].T
    left_back = back[...].T
    lefts[0] = left
    lefts[1] = left_back
    lefts[2] = far_front.T
    message[:width] = dot(left_back, far_front).astype(message.dtype)
    message[width:] = front[pl.ds(pl.multiple_of(where[1] * share, share), share)]
    partial[0] = dot(left, mine[...])
    partial[1] = dot(left, back[...])
    partial[2] = dot(left, far_front)


def near_messages(where, lefts, back, front, *refs):
    number = len(refs) // 2
    near, messages = refs[:number], refs[number:]
    width = lefts.shape[1]
    share = messages[0].shape[0] - width
    for t in range(number):
        ahead = t % 2 == 0
        block = dot(lefts[1 if ahead else 2], near[t ^ 1][...])
        device = where[3 + (t ^ 1)]
        source = back if ahead else front
        messages[t][:width] = block.T.astype(messages[t].dtype)
        messages[t][width:] = source[pl.ds(pl.multiple_of(device * share, share), share)]


def own_blocks(lefts, early, *refs):
    *near, _, partial = refs
    partial[:3] = early[...]
    for t, block in enumerate(near):
        partial[3 + t] = dot(lefts[0], block[...])


def place_blocks(scale, where, odd, *refs):
    own, own_other, far, far_other, gram = refs
    half, width = own.shape[1:]
    first = own.shape[0]
    for side, (near, distant) in enumerate(((own, far), (own_other, far_other))):
        rows = pl.ds(pl.multiple_of((odd[0] ^ side) * half, half), half)
        for t in range(first + far.shape[0]):
            block = near[t] if t < first else distant[t - first]
            if len(gram.shape) == 2:
                start = pl.multiple_of(where[t] * width, width)
                gram[rows, pl.ds(start, width)] = block * scale
            else:
                gram[where[t], rows] = block * scale


def filtered_rows(number, where, mine, *refs):
    blocks, messages, rowwise = (mine,) + refs[:number], refs[number:-1], refs[-1]
    width = mine.shape[1]
    share = rowwise.shape[-2]
    start = pl.multiple_of(where[0] * share, share)
    for t, block in enumerate(blocks):
        rowwise[columns_at(rowwise, where[t], width)] = block[pl.ds(start, share)]
    for t, message in enumerate(messages):
        rowwise[columns_at(rowwise, where[1 + number + t], width)] = message[width:]


def ring_of(size):
    return list(range(0, size, 2)) + list(range(size - 1, 0, -2))


def gram_and_rows(mine):
    size = lax.axis_size("cols")
    device = lax.axis_index("cols")
    assert size % 4 == 0
    reach = size // 4
    order = ring_of(size)
    rows, width = mine.shape
    share = rows // size

    def move(value, by):
        return lax.ppermute(
            value, "cols", [(order[i], order[(i + by) % size]) for i in range(size)]
        )

    distances = [reach] + list(range(1, reach))
    fetched = {by: move(mine, by) for t in distances for by in (t, -t)}
    blocks = [fetched[by] for t in distances for by in (t, -t)]
    sends = [-reach] + [by for t in range(1, reach) for by in (t, -t)]
    steps = [0] + [by for t in distances for by in (-t, t)]
    steps += [-(by + reach) if by > 0 else reach - by for by in sends]

    place = jnp.where(device % 2 == 0, device // 2, size - 1 - device // 2)
    where = (place + jnp.array(steps, jnp.int32)) % size
    where = jnp.where(where < size // 2, 2 * where, 2 * (size - 1 - where) + 1)

    message = jax.ShapeDtypeStruct((width + share, width), mine.dtype)
    early, lefts, far_message = pl.pallas_call(
        early_gram,
        out_shape=(
            jax.ShapeDtypeStruct((3, width, width), jnp.float32),
            jax.ShapeDtypeStruct((3, width, rows), mine.dtype),
            message,
        ),
        in_specs=[SMEM] + [VMEM] * 3,
        out_specs=(VMEM,) * 3,
        compiler_params=params(16),
    )(where, mine, *blocks[:2])
    near = blocks[2:]
    messages = pl.pallas_call(
        near_messages,
        out_shape=(message,) * len(near),
        in_specs=[SMEM] + [VMEM] * (3 + len(near)),
        out_specs=(VMEM,) * len(near),
        compiler_params=params(16),
    )(where, lefts, *blocks)
    own = pl.pallas_call(
        own_blocks,
        out_shape=jax.ShapeDtypeStruct((1 + len(blocks), width, width), jnp.float32),
        in_specs=[VMEM] * (2 + len(near)) + [ANY],
        out_specs=VMEM,
        compiler_params=params(16),
    )(lefts, early, *near, messages[-1])
    messages = [move(value, by) for value, by in zip((far_message, *messages), sends)]
    own, messages = lax.optimization_barrier((sum_of_cores(own), messages))
    far = jnp.stack([message[:width] for message in messages]).astype(jnp.float32)

    flat = width % 128 == 0
    shape = (lambda n: (n, size * width)) if flat else (lambda n: (size, n, width))
    far = sum_of_cores(far)
    rowwise = pl.pallas_call(
        functools.partial(filtered_rows, len(blocks)),
        out_shape=jax.ShapeDtypeStruct(shape(share), mine.dtype),
        in_specs=[SMEM] + [VMEM] * (1 + len(blocks) + len(messages)),
        out_specs=VMEM,
        compiler_params=params(16),
    )(where, mine, *blocks, *messages)
    own = sum_of_chips(own)
    far = sum_of_chips(far)
    gram = pl.pallas_call(
        functools.partial(place_blocks, 1.0 / (rows * lax.axis_size("rows"))),
        out_shape=jax.ShapeDtypeStruct(shape(width), jnp.float32),
        in_specs=[SMEM] * 2 + [VMEM] * 4,
        out_specs=VMEM,
        compiler_params=params(16),
    )(where, (lax.axis_index("rows") & 1)[None], own, with_core(own), far, with_core(far))
    if not flat:
        gram = gram.transpose(1, 0, 2).reshape(width, size * width)
        rowwise = rowwise.transpose(1, 0, 2).reshape(share, size * width)
    return rowwise, gram


def sum_of_cores(blocks):
    odd = lax.axis_index("rows") & 1
    half = blocks.shape[1] // 2
    keep = lax.dynamic_slice_in_dim(blocks, odd * half, half, 1)
    give = lax.dynamic_slice_in_dim(blocks, (1 - odd) * half, half, 1)
    return (keep + with_core(give)).astype(jnp.bfloat16)


def sum_of_chips(sent):
    size = lax.axis_size("rows")
    total = sent.astype(jnp.float32)
    bit = 2
    while bit < size:
        got = lax.ppermute(sent, "rows", [(i, i ^ bit) for i in range(size)])
        total = sent.astype(jnp.float32) + got.astype(jnp.float32)
        sent = total.astype(jnp.bfloat16)
        bit *= 2
    return total


def per_device(search_vectors, tile_values, block_columns):
    row_part = lax.axis_index("rows")
    col_parts = lax.axis_size("cols")
    count, tile, depth = tile_values.shape
    kt = block_columns.shape[1]
    assert REACH == count
    share = search_vectors.shape[0]
    width = search_vectors.shape[1] // col_parts
    rows = share * col_parts
    second = with_chip(tile_values)
    lanes = width % 128 == 0
    pieces = pl.pallas_call(
        copy_columns if lanes else split_columns,
        out_shape=jax.ShapeDtypeStruct((col_parts, share, width), search_vectors.dtype),
        in_specs=[pl.BlockSpec(memory_space=pltpu.HBM) if lanes else VMEM],
        out_specs=pl.BlockSpec(memory_space=pltpu.HBM) if lanes else VMEM,
        scratch_shapes=[pltpu.SemaphoreType.DMA((col_parts,))] if lanes else [],
        compiler_params=params(4),
    )(search_vectors)
    columns = lax.all_to_all(pieces, "cols", split_axis=0, concat_axis=0, tiled=True)
    columns = columns.reshape(rows, width)

    size = HALO * tile
    odd = row_part & 1
    block_columns = block_columns.T
    inner = jnp.arange(count, dtype=jnp.int32)

    def offsets_of(columns, part):
        return jnp.clip(columns - (part * count + inner), -HALO, HALO)

    scratch = [
        pltpu.VMEM((HALO, kt + 1, tile, 2 * tile), jnp.bfloat16),
        pltpu.SMEM((HALO, 2 * HALO + 1), jnp.int32),
    ]
    bands, to_first, sent_columns = pl.pallas_call(
        own_bands,
        out_shape=(
            jax.ShapeDtypeStruct((count // HALO, size, SPAN * size), jnp.bfloat16),
            jax.ShapeDtypeStruct((TILES_REACH, tile, depth), jnp.bfloat16),
            jax.ShapeDtypeStruct((kt, count), jnp.int32),
        ),
        in_specs=[SMEM, SMEM, VMEM, VMEM, ANY],
        out_specs=(VMEM,) * 3,
        scratch_shapes=scratch,
        compiler_params=params(16),
    )(odd[None], offsets_of(block_columns, row_part), block_columns, tile_values, pieces)
    first = with_core(to_first)
    at_first = with_core(sent_columns)
    at_second = with_chip(sent_columns)
    edges = pl.pallas_call(
        edge_bands,
        out_shape=jax.ShapeDtypeStruct(
            (2 * TILES_REACH // HALO, size, SPAN * size), jnp.bfloat16
        ),
        in_specs=[SMEM] * 3 + [VMEM] * 2,
        out_specs=VMEM,
        scratch_shapes=scratch,
        compiler_params=params(16),
    )(
        odd[None],
        offsets_of(at_first, row_part ^ 1),
        offsets_of(at_second, row_part - 1 + 2 * odd),
        first,
        second,
    )
    x_second = with_chip(columns)
    x_first = with_core(columns)

    window = [
        pltpu.VMEM((3 * rows, width), dtype)
        for dtype in (jnp.bfloat16, jnp.bfloat16, jnp.float32, jnp.float32)
    ]
    now, last, sent = pl.pallas_call(
        first_stage,
        out_shape=(
            jax.ShapeDtypeStruct((rows, width), jnp.float32),
            jax.ShapeDtypeStruct((rows + 2 * size, width), jnp.float32),
            jax.ShapeDtypeStruct((2 * rows - 2 * size, width), jnp.bfloat16),
        ),
        in_specs=[SMEM] + [VMEM] * 5,
        out_specs=(VMEM,) * 3,
        scratch_shapes=window,
        compiler_params=params(24),
    )(odd[None], bands, edges, x_first, columns, x_second)
    got_second = with_chip(sent)
    got_first = with_core(sent)
    filtered = pl.pallas_call(
        second_stage,
        out_shape=jax.ShapeDtypeStruct((rows, width), jnp.bfloat16),
        in_specs=[SMEM] + [VMEM] * 6,
        out_specs=VMEM,
        scratch_shapes=window,
        compiler_params=params(24),
    )(odd[None], bands, edges, now, last, got_first, got_second)

    return gram_and_rows(filtered)


def solution(mesh):
    return jax.shard_map(
        per_device,
        mesh=mesh,
        in_specs=(P(("rows", "cols"), None), P("rows", None, None), P("rows", None)),
        out_specs=(P(("rows", "cols"), None), P("cols", None)),
        check_vma=False,
    )
```

```python
import functools

import functools

import jax
import jax.numpy as jnp
from jax import lax
from jax.experimental import pallas as pl
from jax.experimental.pallas import tpu as pltpu
from jax.sharding import PartitionSpec as P

HALO = 4
DEGREE = 8
STAGE = 4
REACH = HALO * STAGE
TILES_REACH = REACH - HALO
SPAN = 3

shift_value = 0.1
half_width = 2.0

SMEM = pl.BlockSpec(memory_space=pltpu.SMEM)
VMEM = pl.BlockSpec(memory_space=pltpu.VMEM)
ANY = pl.BlockSpec(memory_space=pl.ANY)


def params(mebibytes):
    return pltpu.CompilerParams(vmem_limit_bytes=mebibytes * 1024 * 1024)


def with_core(value):
    return lax.ppermute(value, "rows", [(i, i ^ 1) for i in range(lax.axis_size("rows"))])


def with_chip(value):
    odds = range(1, lax.axis_size("rows") - 1, 2)
    return lax.ppermute(value, "rows", [p for k in odds for p in ((k, k + 1), (k + 1, k))])


def place_group(offsets, ahead, tiles, start, bands, band, doubled, slot):
    kt = offsets.shape[0]
    tile = tiles.shape[1]
    blank = kt
    nothing = jnp.zeros((tile, tile), doubled.dtype)
    for i in range(HALO):
        values = tiles[start + i]
        for k in range(kt):
            one = values[:, k * tile:(k + 1) * tile]
            doubled[i, k] = jnp.concatenate([one, one], axis=1)
        for place in range(2 * HALO + 1):
            slot[i, place] = blank
        for k in range(kt):
            slot[i, offsets[k, ahead + start + i] + HALO] = k
    for i in range(HALO):
        rows = slice(i * tile, (i + 1) * tile)
        for pair in range(SPAN * HALO // 2):
            halves = []
            for side in range(2):
                place = 2 * pair + side - i
                if 0 <= place <= 2 * HALO:
                    both = doubled[i, slot[i, place]]
                    halves.append(both[:, side * tile:(side + 1) * tile])
                else:
                    halves.append(nothing)
            columns = slice(2 * pair * tile, 2 * (pair + 1) * tile)
            bands[band, rows, columns] = jnp.concatenate(halves, axis=1)


def clear(doubled):
    doubled[:, doubled.shape[1] - 1] = jnp.zeros(
        doubled.shape[:1] + doubled.shape[2:], doubled.dtype
    )


def place_group(offsets, ahead, tiles, start, bands, band, doubled, slot):
    kt = offsets.shape[0]
    tile = tiles.shape[1]
    blank = kt
    nothing = jnp.zeros((tile, tile), doubled.dtype)
    for i in range(HALO):
        values = tiles[start + i]
        for k in range(kt):
            one = values[:, k * tile:(k + 1) * tile]
            doubled[i, k] = jnp.concatenate([one, one], axis=1)
        for place in range(2 * HALO + 1):
            slot[i, place] = blank
        for k in range(kt):
            slot[i, offsets[k, ahead + start + i] + HALO] = k
    for i in range(HALO):
        rows = slice(i * tile, (i + 1) * tile)
        for pair in range(SPAN * HALO // 2):
            halves = []
            for side in range(2):
                place = 2 * pair + side - i
                if 0 <= place <= 2 * HALO:
                    both = doubled[i, slot[i, place]]
                    halves.append(both[:, side * tile:(side + 1) * tile])
                else:
                    halves.append(nothing)
            columns = slice(2 * pair * tile, 2 * (pair + 1) * tile)
            bands[band, rows, columns] = jnp.concatenate(halves, axis=1)


def clear(doubled):
    doubled[:, doubled.shape[1] - 1] = jnp.zeros(
        doubled.shape[:1] + doubled.shape[2:], doubled.dtype
    )


def split_columns(vectors, pieces):
    width = pieces.shape[2]
    for i in range(pieces.shape[0]):
        pieces[i] = vectors[:, i * width:(i + 1) * width]


def copy_columns(vectors, pieces, done):
    width = pieces.shape[2]
    copies = [
        pltpu.make_async_copy(
            vectors.at[:, i * width:(i + 1) * width], pieces.at[i], done.at[i]
        )
        for i in range(pieces.shape[0])
    ]
    for copy in copies:
        copy.start()
    for copy in copies:
        copy.wait()


def own_bands(odd, offsets, columns, tiles, bands, to_first, columns_out, doubled, slot):
    count = tiles.shape[0]
    sent = to_first.shape[0]
    to_first[...] = tiles[pl.ds((1 - odd[0]) * (count - sent), sent)]
    columns_out[...] = columns[...]
    clear(doubled)

    @pl.loop(0, count // HALO)
    def _(g):
        place_group(offsets, 0, tiles, g * HALO, bands, g, doubled, slot)


def edge_bands(odd, at_first, at_second, first, second, bands, doubled, slot):
    count = at_first.shape[1]
    edge = TILES_REACH // HALO
    clear(doubled)
    for offsets, tiles, behind in ((at_first, first, odd[0]), (at_second, second, 1 - odd[0])):
        begin = behind * (count - TILES_REACH)
        band = (1 - behind) * edge
        skipped = begin * (tiles.shape[0] // count)

        @pl.loop(0, edge)
        def _(g, offsets=offsets, tiles=tiles, begin=begin, band=band, skipped=skipped):
            place_group(offsets, begin - skipped, tiles, skipped + g * HALO, bands, band + g,
                        doubled, slot)


def run_steps(own, edges, w, y, degree):
    middle, size, span = own.shape
    edge = edges.shape[0] // 2
    bands = [edges.at[j] for j in range(edge)]
    bands += [own.at[j] for j in range(middle)]
    bands += [edges.at[edge + j] for j in range(edge)]
    groups = len(bands)
    cur, new = y
    src, dst = w
    for step in range(STAGE):
        for j in range(step, groups - step):
            start = j * size
            here = slice(start + size, start + 2 * size)
            product = dot(bands[j][...], src[start:start + span])
            if degree + step == 0:
                value = (product - shift_value * src[here].astype(jnp.float32)) / half_width
            elif degree + step == 1:
                value = product - shift_value * cur[here] - dst[here].astype(jnp.float32)
            else:
                value = product - shift_value * cur[here] - new[here]
            new[here] = value
            dst[here] = value.astype(jnp.bfloat16)
        cur, new = new, cur
        src, dst = dst, src
    return cur, new, src


def placed(behind, rows):
    return pl.multiple_of((1 - behind) * 2 * rows, rows)


def first_stage(odd, own, edges, x_first, x_own, x_second, now_out, last_out, sent_out,
                w0, w1, y0, y1):
    rows = x_own.shape[0]
    size = own.shape[1]
    starts = (placed(odd[0], rows), rows, placed(1 - odd[0], rows))
    for start, ref in zip(starts, (x_first, x_own, x_second)):
        w0[pl.ds(start, rows)] = ref[...]
    cur, prev, rounded = run_steps(own, edges, (w0, w1), (y0, y1), 0)
    now_out[...] = cur[rows:2 * rows]
    last_out[...] = prev[rows - size:2 * rows + size]
    sent_out[:rows] = rounded[rows:2 * rows]
    sent_out[rows:] = prev[rows + size:2 * rows - size].astype(jnp.bfloat16)


def second_stage(odd, own, edges, now, last, got_first, got_second, out, w0, w1, y0, y1):
    rows = now.shape[0]
    size = own.shape[1]
    here = slice(rows, 2 * rows)
    w0[here] = now[...].astype(jnp.bfloat16)
    y0[here] = now[...]
    y1[rows - size:2 * rows + size] = last[...]
    for got, behind in ((got_first, odd[0]), (got_second, 1 - odd[0])):
        start = placed(behind, rows)
        w0[pl.ds(start, rows)] = got[:rows]
        y0[pl.ds(start, rows)] = got[:rows].astype(jnp.float32)
        y1[pl.ds(pl.multiple_of(start + size, size), rows - 2 * size)] = (
            got[rows:].astype(jnp.float32)
        )
    _, _, rounded = run_steps(own, edges, (w0, w1), (y0, y1), STAGE)
    out[...] = rounded[here]


def dot(a, b):
    return jnp.dot(a, b, preferred_element_type=jnp.float32)


def columns_at(ref, group, width):
    if len(ref.shape) == 2:
        return slice(None), pl.ds(pl.multiple_of(group * width, width), width)
    return (group,)


def early_gram(mine, *refs):
    *blocks, partial, lefts = refs
    left = mine[...].T
    lefts[0] = left
    for t, ref in enumerate((mine, *blocks)):
        block = ref[...]
        if t:
            lefts[t] = block.T
        partial[t] = dot(left, block)


def far_messages(where, lefts, back, front, *messages):
    width = lefts.shape[1]
    share = messages[0].shape[0] - width
    reach = lefts.shape[0] // 2 + 1
    far_back, far_front = back[...], front[...]
    made = []
    for t in range(1, reach):
        made.append((dot(lefts[2 * t], far_back), back, where[2 * t]))
        made.append((dot(lefts[2 * t - 1], far_front), front, where[2 * t - 1]))
    made.append((dot(far_back.T, far_front), front, where[2 * reach - 1]))
    for message, (block, source, device) in zip(messages, made):
        message[:width] = block.astype(message.dtype)
        message[width:] = source[pl.ds(pl.multiple_of(device * share, share), share)]


def own_blocks(lefts, early, back, front, _, partial):
    held = early.shape[0]
    partial[:held] = early[...]
    partial[held] = dot(lefts[0], back[...])
    partial[held + 1] = dot(lefts[0], front[...])


def place_blocks(scale, where, odd, *refs):
    own, own_other, far, far_other, gram = refs
    half, width = own.shape[1:]
    first = own.shape[0]
    for side, (near, distant) in enumerate(((own, far), (own_other, far_other))):
        rows = pl.ds(pl.multiple_of((odd[0] ^ side) * half, half), half)
        for t in range(first + far.shape[0]):
            block = near[t] if t < first else distant[t - first]
            if len(gram.shape) == 2:
                start = pl.multiple_of(where[t] * width, width)
                gram[rows, pl.ds(start, width)] = block * scale
            else:
                gram[where[t], rows] = block * scale


def filtered_rows(number, where, mine, *refs):
    blocks, messages, rowwise = (mine,) + refs[:number], refs[number:-1], refs[-1]
    width = mine.shape[1]
    share = rowwise.shape[-2]
    start = pl.multiple_of(where[0] * share, share)
    for t, block in enumerate(blocks):
        rowwise[columns_at(rowwise, where[t], width)] = block[pl.ds(start, share)]
    for t, message in enumerate(messages):
        rowwise[columns_at(rowwise, where[1 + number + t], width)] = message[width:]


def ring_of(size):
    return list(range(0, size, 2)) + list(range(size - 1, 0, -2))


def gram_and_rows(mine):
    size = lax.axis_size("cols")
    device = lax.axis_index("cols")
    assert size % 4 == 0
    reach = size // 4
    order = ring_of(size)
    rows, width = mine.shape
    share = rows // size

    def move(value, by):
        return lax.ppermute(
            value, "cols", [(order[i], order[(i + by) % size]) for i in range(size)]
        )

    fetched = {by: move(mine, by) for t in range(reach, 0, -1) for by in (t, -t)}
    blocks, steps = [], [0]
    for t in range(1, reach + 1):
        blocks += [fetched[t], fetched[-t]]
        steps += [-t, t]
    sends = [by for t in range(1, reach) for by in (t, -t)] + [-reach]
    steps += [-(by + reach) if by > 0 else reach - by for by in sends]

    place = jnp.where(device % 2 == 0, device // 2, size - 1 - device // 2)
    where = (place + jnp.array(steps, jnp.int32)) % size
    where = jnp.where(where < size // 2, 2 * where, 2 * (size - 1 - where) + 1)

    held = 2 * reach - 1
    early, lefts = pl.pallas_call(
        early_gram,
        out_shape=(
            jax.ShapeDtypeStruct((held, width, width), jnp.float32),
            jax.ShapeDtypeStruct((held, width, rows), mine.dtype),
        ),
        in_specs=[VMEM] * held,
        out_specs=(VMEM, VMEM),
        compiler_params=params(16),
    )(mine, *blocks[:-2])
    message = jax.ShapeDtypeStruct((width + share, width), mine.dtype)
    messages = pl.pallas_call(
        far_messages,
        out_shape=(message,) * len(sends),
        in_specs=[SMEM] + [VMEM] * 3,
        out_specs=(VMEM,) * len(sends),
        compiler_params=params(16),
    )(where, lefts, *blocks[-2:])
    own = pl.pallas_call(
        own_blocks,
        out_shape=jax.ShapeDtypeStruct((held + 2, width, width), jnp.float32),
        in_specs=[VMEM] * 4 + [ANY],
        out_specs=VMEM,
        compiler_params=params(16),
    )(lefts, early, *blocks[-2:], messages[-1])
    messages = [move(value, by) for value, by in zip(messages, sends)]
    own, messages = lax.optimization_barrier((sum_of_cores(own), messages))
    far = jnp.stack([message[:width] for message in messages]).astype(jnp.float32)

    flat = width % 128 == 0
    shape = (lambda n: (n, size * width)) if flat else (lambda n: (size, n, width))
    far = sum_of_cores(far)
    rowwise = pl.pallas_call(
        functools.partial(filtered_rows, len(blocks)),
        out_shape=jax.ShapeDtypeStruct(shape(share), mine.dtype),
        in_specs=[SMEM] + [VMEM] * (1 + len(blocks) + len(messages)),
        out_specs=VMEM,
        compiler_params=params(16),
    )(where, mine, *blocks, *messages)
    own = sum_of_chips(own)
    far = sum_of_chips(far)
    gram = pl.pallas_call(
        functools.partial(place_blocks, 1.0 / (rows * lax.axis_size("rows"))),
        out_shape=jax.ShapeDtypeStruct(shape(width), jnp.float32),
        in_specs=[SMEM] * 2 + [VMEM] * 4,
        out_specs=VMEM,
        compiler_params=params(16),
    )(where, (lax.axis_index("rows") & 1)[None], own, with_core(own), far, with_core(far))
    if not flat:
        gram = gram.transpose(1, 0, 2).reshape(width, size * width)
        rowwise = rowwise.transpose(1, 0, 2).reshape(share, size * width)
    return rowwise, gram


def sum_of_cores(blocks):
    odd = lax.axis_index("rows") & 1
    half = blocks.shape[1] // 2
    keep = lax.dynamic_slice_in_dim(blocks, odd * half, half, 1)
    give = lax.dynamic_slice_in_dim(blocks, (1 - odd) * half, half, 1)
    return (keep + with_core(give)).astype(jnp.bfloat16)


def sum_of_chips(sent):
    size = lax.axis_size("rows")
    total = sent.astype(jnp.float32)
    bit = 2
    while bit < size:
        got = lax.ppermute(sent, "rows", [(i, i ^ bit) for i in range(size)])
        total = sent.astype(jnp.float32) + got.astype(jnp.float32)
        sent = total.astype(jnp.bfloat16)
        bit *= 2
    return total


def per_device(search_vectors, tile_values, block_columns):
    row_part = lax.axis_index("rows")
    col_parts = lax.axis_size("cols")
    count, tile, depth = tile_values.shape
    kt = block_columns.shape[1]
    assert REACH == count
    share = search_vectors.shape[0]
    width = search_vectors.shape[1] // col_parts
    rows = share * col_parts
    second = with_chip(tile_values)
    columns = lax.all_to_all(search_vectors, "cols", split_axis=1, concat_axis=0, tiled=True)

    size = HALO * tile
    odd = row_part & 1
    block_columns = block_columns.T
    inner = jnp.arange(count, dtype=jnp.int32)

    def offsets_of(columns, part):
        return jnp.clip(columns - (part * count + inner), -HALO, HALO)

    scratch = [
        pltpu.VMEM((HALO, kt + 1, tile, 2 * tile), jnp.bfloat16),
        pltpu.SMEM((HALO, 2 * HALO + 1), jnp.int32),
    ]
    bands, to_first, sent_columns = pl.pallas_call(
        own_bands,
        out_shape=(
            jax.ShapeDtypeStruct((count // HALO, size, SPAN * size), jnp.bfloat16),
            jax.ShapeDtypeStruct((TILES_REACH, tile, depth), jnp.bfloat16),
            jax.ShapeDtypeStruct((kt, count), jnp.int32),
        ),
        in_specs=[SMEM, SMEM, VMEM, VMEM],
        out_specs=(VMEM,) * 3,
        scratch_shapes=scratch,
        compiler_params=params(16),
    )(odd[None], offsets_of(block_columns, row_part), block_columns, tile_values)
    first = with_core(to_first)
    at_first = with_core(sent_columns)
    at_second = with_chip(sent_columns)
    edges = pl.pallas_call(
        edge_bands,
        out_shape=jax.ShapeDtypeStruct(
            (2 * TILES_REACH // HALO, size, SPAN * size), jnp.bfloat16
        ),
        in_specs=[SMEM] * 3 + [VMEM] * 2,
        out_specs=VMEM,
        scratch_shapes=scratch,
        compiler_params=params(16),
    )(
        odd[None],
        offsets_of(at_first, row_part ^ 1),
        offsets_of(at_second, row_part - 1 + 2 * odd),
        first,
        second,
    )
    x_second = with_chip(columns)
    x_first = with_core(columns)

    window = [
        pltpu.VMEM((3 * rows, width), dtype)
        for dtype in (jnp.bfloat16, jnp.bfloat16, jnp.float32, jnp.float32)
    ]
    now, last, sent = pl.pallas_call(
        first_stage,
        out_shape=(
            jax.ShapeDtypeStruct((rows, width), jnp.float32),
            jax.ShapeDtypeStruct((rows + 2 * size, width), jnp.float32),
            jax.ShapeDtypeStruct((2 * rows - 2 * size, width), jnp.bfloat16),
        ),
        in_specs=[SMEM] + [VMEM] * 5,
        out_specs=(VMEM,) * 3,
        scratch_shapes=window,
        compiler_params=params(24),
    )(odd[None], bands, edges, x_first, columns, x_second)
    got_second = with_chip(sent)
    got_first = with_core(sent)
    filtered = pl.pallas_call(
        second_stage,
        out_shape=jax.ShapeDtypeStruct((rows, width), jnp.bfloat16),
        in_specs=[SMEM] + [VMEM] * 6,
        out_specs=VMEM,
        scratch_shapes=window,
        compiler_params=params(24),
    )(odd[None], bands, edges, now, last, got_first, got_second)

    return gram_and_rows(filtered)


def solution(mesh):
    return jax.shard_map(
        per_device,
        mesh=mesh,
        in_specs=(P(("rows", "cols"), None), P("rows", None, None), P("rows", None)),
        out_specs=(P(("rows", "cols"), None), P("cols", None)),
        check_vma=False,
    )
```

```python
import functools

import functools

import jax
import jax.numpy as jnp
from jax import lax
from jax.experimental import pallas as pl
from jax.experimental.pallas import tpu as pltpu
from jax.sharding import PartitionSpec as P

HALO = 4
DEGREE = 8
STAGE = 4
REACH = HALO * STAGE
TILES_REACH = REACH - HALO
SPAN = 3

shift_value = 0.1
half_width = 2.0

SMEM = pl.BlockSpec(memory_space=pltpu.SMEM)
VMEM = pl.BlockSpec(memory_space=pltpu.VMEM)
ANY = pl.BlockSpec(memory_space=pl.ANY)


def params(mebibytes):
    return pltpu.CompilerParams(vmem_limit_bytes=mebibytes * 1024 * 1024)


def with_core(value):
    return lax.ppermute(value, "rows", [(i, i ^ 1) for i in range(lax.axis_size("rows"))])


def with_chip(value):
    odds = range(1, lax.axis_size("rows") - 1, 2)
    return lax.ppermute(value, "rows", [p for k in odds for p in ((k, k + 1), (k + 1, k))])


def place_group(offsets, ahead, tiles, start, bands, band, doubled, slot):
    kt = offsets.shape[0]
    tile = tiles.shape[1]
    blank = kt
    nothing = jnp.zeros((tile, tile), doubled.dtype)
    for i in range(HALO):
        values = tiles[start + i]
        for k in range(kt):
            one = values[:, k * tile:(k + 1) * tile]
            doubled[i, k] = jnp.concatenate([one, one], axis=1)
        for place in range(2 * HALO + 1):
            slot[i, place] = blank
        for k in range(kt):
            slot[i, offsets[k, ahead + start + i] + HALO] = k
    for i in range(HALO):
        rows = slice(i * tile, (i + 1) * tile)
        for pair in range(SPAN * HALO // 2):
            halves = []
            for side in range(2):
                place = 2 * pair + side - i
                if 0 <= place <= 2 * HALO:
                    both = doubled[i, slot[i, place]]
                    halves.append(both[:, side * tile:(side + 1) * tile])
                else:
                    halves.append(nothing)
            columns = slice(2 * pair * tile, 2 * (pair + 1) * tile)
            bands[band, rows, columns] = jnp.concatenate(halves, axis=1)


def clear(doubled):
    doubled[:, doubled.shape[1] - 1] = jnp.zeros(
        doubled.shape[:1] + doubled.shape[2:], doubled.dtype
    )


def place_group(offsets, ahead, tiles, start, bands, band, doubled, slot):
    kt = offsets.shape[0]
    tile = tiles.shape[1]
    blank = kt
    nothing = jnp.zeros((tile, tile), doubled.dtype)
    for i in range(HALO):
        values = tiles[start + i]
        for k in range(kt):
            one = values[:, k * tile:(k + 1) * tile]
            doubled[i, k] = jnp.concatenate([one, one], axis=1)
        for place in range(2 * HALO + 1):
            slot[i, place] = blank
        for k in range(kt):
            slot[i, offsets[k, ahead + start + i] + HALO] = k
    for i in range(HALO):
        rows = slice(i * tile, (i + 1) * tile)
        for pair in range(SPAN * HALO // 2):
            halves = []
            for side in range(2):
                place = 2 * pair + side - i
                if 0 <= place <= 2 * HALO:
                    both = doubled[i, slot[i, place]]
                    halves.append(both[:, side * tile:(side + 1) * tile])
                else:
                    halves.append(nothing)
            columns = slice(2 * pair * tile, 2 * (pair + 1) * tile)
            bands[band, rows, columns] = jnp.concatenate(halves, axis=1)


def clear(doubled):
    doubled[:, doubled.shape[1] - 1] = jnp.zeros(
        doubled.shape[:1] + doubled.shape[2:], doubled.dtype
    )


def split_columns(vectors, pieces):
    width = pieces.shape[2]
    for i in range(pieces.shape[0]):
        pieces[i] = vectors[:, i * width:(i + 1) * width]


def copy_columns(vectors, pieces, done):
    width = pieces.shape[2]
    copies = [
        pltpu.make_async_copy(
            vectors.at[:, i * width:(i + 1) * width], pieces.at[i], done.at[i]
        )
        for i in range(pieces.shape[0])
    ]
    for copy in copies:
        copy.start()
    for copy in copies:
        copy.wait()


def own_bands(odd, offsets, to_send, tiles, bands, to_first, offsets_out, doubled, slot):
    count = tiles.shape[0]
    sent = to_first.shape[0]
    to_first[...] = tiles[pl.ds((1 - odd[0]) * (count - sent), sent)]
    offsets_out[...] = to_send[...]
    clear(doubled)

    @pl.loop(0, count // HALO)
    def _(g):
        place_group(offsets, 0, tiles, g * HALO, bands, g, doubled, slot)


def edge_bands(odd, at_first, at_second, first, second, bands, doubled, slot):
    count = at_first.shape[1]
    edge = TILES_REACH // HALO
    clear(doubled)
    for offsets, tiles, behind in ((at_first, first, odd[0]), (at_second, second, 1 - odd[0])):
        begin = behind * (count - TILES_REACH)
        band = (1 - behind) * edge
        skipped = begin * (tiles.shape[0] // count)

        @pl.loop(0, edge)
        def _(g, offsets=offsets, tiles=tiles, begin=begin, band=band, skipped=skipped):
            place_group(offsets, begin - skipped, tiles, skipped + g * HALO, bands, band + g,
                        doubled, slot)


def run_steps(own, edges, w, y, degree):
    middle, size, span = own.shape
    edge = edges.shape[0] // 2
    bands = [edges.at[j] for j in range(edge)]
    bands += [own.at[j] for j in range(middle)]
    bands += [edges.at[edge + j] for j in range(edge)]
    groups = len(bands)
    cur, new = y
    src, dst = w
    for step in range(STAGE):
        for j in range(step, groups - step):
            start = j * size
            here = slice(start + size, start + 2 * size)
            product = dot(bands[j][...], src[start:start + span])
            if degree + step == 0:
                value = (product - shift_value * src[here].astype(jnp.float32)) / half_width
            elif degree + step == 1:
                value = product - shift_value * cur[here] - dst[here].astype(jnp.float32)
            else:
                value = product - shift_value * cur[here] - new[here]
            new[here] = value
            dst[here] = value.astype(jnp.bfloat16)
        cur, new = new, cur
        src, dst = dst, src
    return cur, new, src


def placed(behind, rows):
    return pl.multiple_of((1 - behind) * 2 * rows, rows)


def first_stage(odd, own, edges, x_first, x_own, x_second, now_out, last_out, sent_out,
                w0, w1, y0, y1):
    rows = x_own.shape[0]
    size = own.shape[1]
    starts = (placed(odd[0], rows), rows, placed(1 - odd[0], rows))
    for start, ref in zip(starts, (x_first, x_own, x_second)):
        w0[pl.ds(start, rows)] = ref[...]
    cur, prev, rounded = run_steps(own, edges, (w0, w1), (y0, y1), 0)
    now_out[...] = cur[rows:2 * rows]
    last_out[...] = prev[rows - size:2 * rows + size]
    sent_out[:rows] = rounded[rows:2 * rows]
    sent_out[rows:] = prev[rows + size:2 * rows - size].astype(jnp.bfloat16)


def second_stage(odd, own, edges, now, last, got_first, got_second, out, w0, w1, y0, y1):
    rows = now.shape[0]
    size = own.shape[1]
    here = slice(rows, 2 * rows)
    w0[here] = now[...].astype(jnp.bfloat16)
    y0[here] = now[...]
    y1[rows - size:2 * rows + size] = last[...]
    for got, behind in ((got_first, odd[0]), (got_second, 1 - odd[0])):
        start = placed(behind, rows)
        w0[pl.ds(start, rows)] = got[:rows]
        y0[pl.ds(start, rows)] = got[:rows].astype(jnp.float32)
        y1[pl.ds(pl.multiple_of(start + size, size), rows - 2 * size)] = (
            got[rows:].astype(jnp.float32)
        )
    _, _, rounded = run_steps(own, edges, (w0, w1), (y0, y1), STAGE)
    out[...] = rounded[here]


def dot(a, b):
    return jnp.dot(a, b, preferred_element_type=jnp.float32)


def columns_at(ref, group, width):
    if len(ref.shape) == 2:
        return slice(None), pl.ds(pl.multiple_of(group * width, width), width)
    return (group,)


def early_gram(mine, *refs):
    *blocks, partial, lefts = refs
    left = mine[...].T
    lefts[0] = left
    for t, ref in enumerate((mine, *blocks)):
        block = ref[...]
        if t:
            lefts[t] = block.T
        partial[t] = dot(left, block)


def far_messages(where, lefts, back, front, *messages):
    width = lefts.shape[1]
    share = messages[0].shape[0] - width
    reach = lefts.shape[0] // 2 + 1
    far_back, far_front = back[...], front[...]
    made = []
    for t in range(1, reach):
        made.append((dot(lefts[2 * t], far_back), back, where[2 * t]))
        made.append((dot(lefts[2 * t - 1], far_front), front, where[2 * t - 1]))
    made.append((dot(far_back.T, far_front), front, where[2 * reach - 1]))
    for message, (block, source, device) in zip(messages, made):
        message[:width] = block.astype(message.dtype)
        message[width:] = source[pl.ds(pl.multiple_of(device * share, share), share)]


def own_blocks(lefts, early, back, front, _, partial):
    held = early.shape[0]
    partial[:held] = early[...]
    partial[held] = dot(lefts[0], back[...])
    partial[held + 1] = dot(lefts[0], front[...])


def place_blocks(scale, where, odd, *refs):
    own, own_other, far, far_other, gram = refs
    half, width = own.shape[1:]
    first = own.shape[0]
    for side, (near, distant) in enumerate(((own, far), (own_other, far_other))):
        rows = pl.ds(pl.multiple_of((odd[0] ^ side) * half, half), half)
        for t in range(first + far.shape[0]):
            block = near[t] if t < first else distant[t - first]
            if len(gram.shape) == 2:
                start = pl.multiple_of(where[t] * width, width)
                gram[rows, pl.ds(start, width)] = block * scale
            else:
                gram[where[t], rows] = block * scale


def filtered_rows(number, where, mine, *refs):
    blocks, messages, rowwise = (mine,) + refs[:number], refs[number:-1], refs[-1]
    width = mine.shape[1]
    share = rowwise.shape[-2]
    start = pl.multiple_of(where[0] * share, share)
    for t, block in enumerate(blocks):
        rowwise[columns_at(rowwise, where[t], width)] = block[pl.ds(start, share)]
    for t, message in enumerate(messages):
        rowwise[columns_at(rowwise, where[1 + number + t], width)] = message[width:]


def ring_of(size):
    return list(range(0, size, 2)) + list(range(size - 1, 0, -2))


def gram_and_rows(mine):
    size = lax.axis_size("cols")
    device = lax.axis_index("cols")
    assert size % 4 == 0
    reach = size // 4
    order = ring_of(size)
    rows, width = mine.shape
    share = rows // size

    def move(value, by):
        return lax.ppermute(
            value, "cols", [(order[i], order[(i + by) % size]) for i in range(size)]
        )

    fetched = {by: move(mine, by) for t in range(reach, 0, -1) for by in (t, -t)}
    blocks, steps = [], [0]
    for t in range(1, reach + 1):
        blocks += [fetched[t], fetched[-t]]
        steps += [-t, t]
    sends = [by for t in range(1, reach) for by in (t, -t)] + [-reach]
    steps += [-(by + reach) if by > 0 else reach - by for by in sends]

    place = jnp.where(device % 2 == 0, device // 2, size - 1 - device // 2)
    where = (place + jnp.array(steps, jnp.int32)) % size
    where = jnp.where(where < size // 2, 2 * where, 2 * (size - 1 - where) + 1)

    held = 2 * reach - 1
    early, lefts = pl.pallas_call(
        early_gram,
        out_shape=(
            jax.ShapeDtypeStruct((held, width, width), jnp.float32),
            jax.ShapeDtypeStruct((held, width, rows), mine.dtype),
        ),
        in_specs=[VMEM] * held,
        out_specs=(VMEM, VMEM),
        compiler_params=params(16),
    )(mine, *blocks[:-2])
    message = jax.ShapeDtypeStruct((width + share, width), mine.dtype)
    messages = pl.pallas_call(
        far_messages,
        out_shape=(message,) * len(sends),
        in_specs=[SMEM] + [VMEM] * 3,
        out_specs=(VMEM,) * len(sends),
        compiler_params=params(16),
    )(where, lefts, *blocks[-2:])
    own = pl.pallas_call(
        own_blocks,
        out_shape=jax.ShapeDtypeStruct((held + 2, width, width), jnp.float32),
        in_specs=[VMEM] * 4 + [ANY],
        out_specs=VMEM,
        compiler_params=params(16),
    )(lefts, early, *blocks[-2:], messages[-1])
    messages = [move(value, by) for value, by in zip(messages, sends)]
    own, messages = lax.optimization_barrier((sum_of_cores(own), messages))
    far = jnp.stack([message[:width] for message in messages]).astype(jnp.float32)

    flat = width % 128 == 0
    shape = (lambda n: (n, size * width)) if flat else (lambda n: (size, n, width))
    far = sum_of_cores(far)
    rowwise = pl.pallas_call(
        functools.partial(filtered_rows, len(blocks)),
        out_shape=jax.ShapeDtypeStruct(shape(share), mine.dtype),
        in_specs=[SMEM] + [VMEM] * (1 + len(blocks) + len(messages)),
        out_specs=VMEM,
        compiler_params=params(16),
    )(where, mine, *blocks, *messages)
    own = sum_of_chips(own)
    far = sum_of_chips(far)
    gram = pl.pallas_call(
        functools.partial(place_blocks, 1.0 / (rows * lax.axis_size("rows"))),
        out_shape=jax.ShapeDtypeStruct(shape(width), jnp.float32),
        in_specs=[SMEM] * 2 + [VMEM] * 4,
        out_specs=VMEM,
        compiler_params=params(16),
    )(where, (lax.axis_index("rows") & 1)[None], own, with_core(own), far, with_core(far))
    if not flat:
        gram = gram.transpose(1, 0, 2).reshape(width, size * width)
        rowwise = rowwise.transpose(1, 0, 2).reshape(share, size * width)
    return rowwise, gram


def sum_of_cores(blocks):
    odd = lax.axis_index("rows") & 1
    half = blocks.shape[1] // 2
    keep = lax.dynamic_slice_in_dim(blocks, odd * half, half, 1)
    give = lax.dynamic_slice_in_dim(blocks, (1 - odd) * half, half, 1)
    return (keep + with_core(give)).astype(jnp.bfloat16)


def sum_of_chips(sent):
    size = lax.axis_size("rows")
    total = sent.astype(jnp.float32)
    bit = 2
    while bit < size:
        got = lax.ppermute(sent, "rows", [(i, i ^ bit) for i in range(size)])
        total = sent.astype(jnp.float32) + got.astype(jnp.float32)
        sent = total.astype(jnp.bfloat16)
        bit *= 2
    return total


def per_device(search_vectors, tile_values, block_columns):
    row_part = lax.axis_index("rows")
    col_parts = lax.axis_size("cols")
    count, tile, depth = tile_values.shape
    kt = block_columns.shape[1]
    assert REACH == count
    share = search_vectors.shape[0]
    width = search_vectors.shape[1] // col_parts
    rows = share * col_parts
    second = with_chip(tile_values)
    columns = lax.all_to_all(search_vectors, "cols", split_axis=1, concat_axis=0, tiled=True)

    size = HALO * tile
    odd = row_part & 1
    block_columns = block_columns.T
    inner = jnp.arange(count, dtype=jnp.int32)

    offsets = block_columns - (row_part * count + inner)

    scratch = [
        pltpu.VMEM((HALO, kt + 1, tile, 2 * tile), jnp.bfloat16),
        pltpu.SMEM((HALO, 2 * HALO + 1), jnp.int32),
    ]
    bands, to_first, sent_offsets = pl.pallas_call(
        own_bands,
        out_shape=(
            jax.ShapeDtypeStruct((count // HALO, size, SPAN * size), jnp.bfloat16),
            jax.ShapeDtypeStruct((TILES_REACH, tile, depth), jnp.bfloat16),
            jax.ShapeDtypeStruct((kt, count), jnp.int32),
        ),
        in_specs=[SMEM, SMEM, VMEM, VMEM],
        out_specs=(VMEM,) * 3,
        scratch_shapes=scratch,
        compiler_params=params(16),
    )(odd[None], offsets, offsets, tile_values)
    first = with_core(to_first)
    at_first = with_core(sent_offsets)
    at_second = with_chip(sent_offsets)
    edges = pl.pallas_call(
        edge_bands,
        out_shape=jax.ShapeDtypeStruct(
            (2 * TILES_REACH // HALO, size, SPAN * size), jnp.bfloat16
        ),
        in_specs=[SMEM] * 3 + [VMEM] * 2,
        out_specs=VMEM,
        scratch_shapes=scratch,
        compiler_params=params(16),
    )(
        odd[None],
        jnp.clip(at_first, -HALO, HALO),
        jnp.clip(at_second, -HALO, HALO),
        first,
        second,
    )
    x_second = with_chip(columns)
    x_first = with_core(columns)

    window = [
        pltpu.VMEM((3 * rows, width), dtype)
        for dtype in (jnp.bfloat16, jnp.bfloat16, jnp.float32, jnp.float32)
    ]
    now, last, sent = pl.pallas_call(
        first_stage,
        out_shape=(
            jax.ShapeDtypeStruct((rows, width), jnp.float32),
            jax.ShapeDtypeStruct((rows + 2 * size, width), jnp.float32),
            jax.ShapeDtypeStruct((2 * rows - 2 * size, width), jnp.bfloat16),
        ),
        in_specs=[SMEM] + [VMEM] * 5,
        out_specs=(VMEM,) * 3,
        scratch_shapes=window,
        compiler_params=params(24),
    )(odd[None], bands, edges, x_first, columns, x_second)
    got_second = with_chip(sent)
    got_first = with_core(sent)
    filtered = pl.pallas_call(
        second_stage,
        out_shape=jax.ShapeDtypeStruct((rows, width), jnp.bfloat16),
        in_specs=[SMEM] + [VMEM] * 6,
        out_specs=VMEM,
        scratch_shapes=window,
        compiler_params=params(24),
    )(odd[None], bands, edges, now, last, got_first, got_second)

    return gram_and_rows(filtered)


def solution(mesh):
    return jax.shard_map(
        per_device,
        mesh=mesh,
        in_specs=(P(("rows", "cols"), None), P("rows", None, None), P("rows", None)),
        out_specs=(P(("rows", "cols"), None), P("cols", None)),
        check_vma=False,
    )
```

```python
import functools

import functools

import jax
import jax.numpy as jnp
from jax import lax
from jax.experimental import pallas as pl
from jax.experimental.pallas import tpu as pltpu
from jax.sharding import PartitionSpec as P

HALO = 4
DEGREE = 8
STAGE = 4
REACH = HALO * STAGE
TILES_REACH = REACH - HALO
SPAN = 3

shift_value = 0.1
half_width = 2.0

SMEM = pl.BlockSpec(memory_space=pltpu.SMEM)
VMEM = pl.BlockSpec(memory_space=pltpu.VMEM)
ANY = pl.BlockSpec(memory_space=pl.ANY)


def params(mebibytes):
    return pltpu.CompilerParams(vmem_limit_bytes=mebibytes * 1024 * 1024)


def with_core(value):
    return lax.ppermute(value, "rows", [(i, i ^ 1) for i in range(lax.axis_size("rows"))])


def with_chip(value):
    odds = range(1, lax.axis_size("rows") - 1, 2)
    return lax.ppermute(value, "rows", [p for k in odds for p in ((k, k + 1), (k + 1, k))])


def place_group(offsets, ahead, tiles, start, bands, band, doubled, slot):
    kt = offsets.shape[0]
    tile = tiles.shape[1]
    blank = kt
    nothing = jnp.zeros((tile, tile), doubled.dtype)
    for i in range(HALO):
        values = tiles[start + i]
        for k in range(kt):
            one = values[:, k * tile:(k + 1) * tile]
            doubled[i, k] = jnp.concatenate([one, one], axis=1)
        for place in range(2 * HALO + 1):
            slot[i, place] = blank
        for k in range(kt):
            slot[i, offsets[k, ahead + start + i] + HALO] = k
    for i in range(HALO):
        rows = slice(i * tile, (i + 1) * tile)
        for pair in range(SPAN * HALO // 2):
            halves = []
            for side in range(2):
                place = 2 * pair + side - i
                if 0 <= place <= 2 * HALO:
                    both = doubled[i, slot[i, place]]
                    halves.append(both[:, side * tile:(side + 1) * tile])
                else:
                    halves.append(nothing)
            columns = slice(2 * pair * tile, 2 * (pair + 1) * tile)
            bands[band, rows, columns] = jnp.concatenate(halves, axis=1)


def clear(doubled):
    doubled[:, doubled.shape[1] - 1] = jnp.zeros(
        doubled.shape[:1] + doubled.shape[2:], doubled.dtype
    )


def place_group(offsets, ahead, tiles, start, bands, band, doubled, slot):
    kt = offsets.shape[0]
    tile = tiles.shape[1]
    blank = kt
    nothing = jnp.zeros((tile, tile), doubled.dtype)
    for i in range(HALO):
        values = tiles[start + i]
        for k in range(kt):
            one = values[:, k * tile:(k + 1) * tile]
            doubled[i, k] = jnp.concatenate([one, one], axis=1)
        for place in range(2 * HALO + 1):
            slot[i, place] = blank
        for k in range(kt):
            slot[i, offsets[k, ahead + start + i] + HALO] = k
    for i in range(HALO):
        rows = slice(i * tile, (i + 1) * tile)
        for pair in range(SPAN * HALO // 2):
            halves = []
            for side in range(2):
                place = 2 * pair + side - i
                if 0 <= place <= 2 * HALO:
                    both = doubled[i, slot[i, place]]
                    halves.append(both[:, side * tile:(side + 1) * tile])
                else:
                    halves.append(nothing)
            columns = slice(2 * pair * tile, 2 * (pair + 1) * tile)
            bands[band, rows, columns] = jnp.concatenate(halves, axis=1)


def clear(doubled):
    doubled[:, doubled.shape[1] - 1] = jnp.zeros(
        doubled.shape[:1] + doubled.shape[2:], doubled.dtype
    )


def split_columns(vectors, pieces):
    width = pieces.shape[2]
    for i in range(pieces.shape[0]):
        pieces[i] = vectors[:, i * width:(i + 1) * width]


def copy_columns(vectors, pieces, done):
    width = pieces.shape[2]
    copies = [
        pltpu.make_async_copy(
            vectors.at[:, i * width:(i + 1) * width], pieces.at[i], done.at[i]
        )
        for i in range(pieces.shape[0])
    ]
    for copy in copies:
        copy.start()
    for copy in copies:
        copy.wait()


def own_bands(odd, offsets, to_send, tiles, bands, to_first, offsets_out, doubled, slot):
    count = tiles.shape[0]
    sent = to_first.shape[0]
    to_first[...] = tiles[pl.ds((1 - odd[0]) * (count - sent), sent)]
    offsets_out[...] = to_send[...]
    clear(doubled)

    @pl.loop(0, count // HALO)
    def _(g):
        place_group(offsets, 0, tiles, g * HALO, bands, g, doubled, slot)


def edge_bands(odd, at_first, at_second, first, second, bands, doubled, slot):
    count = at_first.shape[1]
    edge = TILES_REACH // HALO
    clear(doubled)
    for offsets, tiles, behind in ((at_first, first, odd[0]), (at_second, second, 1 - odd[0])):
        begin = behind * (count - TILES_REACH)
        band = (1 - behind) * edge
        skipped = begin * (tiles.shape[0] // count)

        @pl.loop(0, edge)
        def _(g, offsets=offsets, tiles=tiles, begin=begin, band=band, skipped=skipped):
            place_group(offsets, begin - skipped, tiles, skipped + g * HALO, bands, band + g,
                        doubled, slot)


def run_steps(own, edges, w, y, degree):
    middle, size, span = own.shape
    edge = edges.shape[0] // 2
    bands = [edges.at[j] for j in range(edge)]
    bands += [own.at[j] for j in range(middle)]
    bands += [edges.at[edge + j] for j in range(edge)]
    groups = len(bands)
    cur, new = y
    src, dst = w
    for step in range(STAGE):
        for j in range(step, groups - step):
            start = j * size
            here = slice(start + size, start + 2 * size)
            product = dot(bands[j][...], src[start:start + span])
            if degree + step == 0:
                value = (product - shift_value * src[here].astype(jnp.float32)) / half_width
            elif degree + step == 1:
                value = product - shift_value * cur[here] - dst[here].astype(jnp.float32)
            else:
                value = product - shift_value * cur[here] - new[here]
            new[here] = value
            dst[here] = value.astype(jnp.bfloat16)
        cur, new = new, cur
        src, dst = dst, src
    return cur, new, src


def placed(behind, rows):
    return pl.multiple_of((1 - behind) * 2 * rows, rows)


def first_stage(odd, own, edges, x_first, x_own, x_second, now_out, last_out, sent_out,
                w0, w1, y0, y1):
    rows = x_own.shape[0]
    size = own.shape[1]
    starts = (placed(odd[0], rows), rows, placed(1 - odd[0], rows))
    for start, ref in zip(starts, (x_first, x_own, x_second)):
        w0[pl.ds(start, rows)] = ref[...]
    cur, prev, rounded = run_steps(own, edges, (w0, w1), (y0, y1), 0)
    now_out[...] = cur[rows:2 * rows]
    last_out[...] = prev[rows - size:2 * rows + size]
    sent_out[:rows] = rounded[rows:2 * rows]
    sent_out[rows:] = prev[rows + size:2 * rows - size].astype(jnp.bfloat16)


def second_stage(odd, own, edges, now, last, got_first, got_second, out, w0, w1, y0, y1):
    rows = now.shape[0]
    size = own.shape[1]
    here = slice(rows, 2 * rows)
    w0[here] = now[...].astype(jnp.bfloat16)
    y0[here] = now[...]
    y1[rows - size:2 * rows + size] = last[...]
    for got, behind in ((got_first, odd[0]), (got_second, 1 - odd[0])):
        start = placed(behind, rows)
        w0[pl.ds(start, rows)] = got[:rows]
        y0[pl.ds(start, rows)] = got[:rows].astype(jnp.float32)
        y1[pl.ds(pl.multiple_of(start + size, size), rows - 2 * size)] = (
            got[rows:].astype(jnp.float32)
        )
    _, _, rounded = run_steps(own, edges, (w0, w1), (y0, y1), STAGE)
    out[...] = rounded[here]


def dot(a, b):
    return jnp.dot(a, b, preferred_element_type=jnp.float32)


def columns_at(ref, group, width):
    if len(ref.shape) == 2:
        return slice(None), pl.ds(pl.multiple_of(group * width, width), width)
    return (group,)


def early_gram(mine, *refs):
    *blocks, partial, lefts = refs
    left = mine[...].T
    lefts[0] = left
    for t, ref in enumerate((mine, *blocks)):
        block = ref[...]
        if t:
            lefts[t] = block.T
        partial[t] = dot(left, block)


def far_messages(where, lefts, back, front, *messages):
    width = lefts.shape[1]
    share = messages[0].shape[0] - width
    reach = lefts.shape[0] // 2 + 1
    far_back, far_front = back[...], front[...]
    made = []
    for t in range(1, reach):
        made.append((dot(lefts[2 * t], far_back), back, where[2 * t]))
        made.append((dot(lefts[2 * t - 1], far_front), front, where[2 * t - 1]))
    made.append((dot(far_back.T, far_front), front, where[2 * reach - 1]))
    for message, (block, source, device) in zip(messages, made):
        message[:width] = block.astype(message.dtype)
        message[width:] = source[pl.ds(pl.multiple_of(device * share, share), share)]


def own_blocks(lefts, early, back, front, _, partial):
    held = early.shape[0]
    partial[:held] = early[...]
    partial[held] = dot(lefts[0], back[...])
    partial[held + 1] = dot(lefts[0], front[...])


def place_blocks(scale, where, odd, *refs):
    own, own_other, far, far_other, gram = refs
    half, width = own.shape[1:]
    first = own.shape[0]
    for side, (near, distant) in enumerate(((own, far), (own_other, far_other))):
        rows = pl.ds(pl.multiple_of((odd[0] ^ side) * half, half), half)
        for t in range(first + far.shape[0]):
            block = near[t] if t < first else distant[t - first]
            if len(gram.shape) == 2:
                start = pl.multiple_of(where[t] * width, width)
                gram[rows, pl.ds(start, width)] = block * scale
            else:
                gram[where[t], rows] = block * scale


def filtered_rows(number, where, mine, *refs):
    blocks, messages, rowwise = (mine,) + refs[:number], refs[number:-1], refs[-1]
    width = mine.shape[1]
    share = rowwise.shape[-2]
    start = pl.multiple_of(where[0] * share, share)
    for t, block in enumerate(blocks):
        rowwise[columns_at(rowwise, where[t], width)] = block[pl.ds(start, share)]
    for t, message in enumerate(messages):
        rowwise[columns_at(rowwise, where[1 + number + t], width)] = message[width:]


def ring_of(size):
    return list(range(0, size, 2)) + list(range(size - 1, 0, -2))


def gram_and_rows(mine):
    size = lax.axis_size("cols")
    device = lax.axis_index("cols")
    assert size % 4 == 0
    reach = size // 4
    order = ring_of(size)
    rows, width = mine.shape
    share = rows // size

    def move(value, by):
        return lax.ppermute(
            value, "cols", [(order[i], order[(i + by) % size]) for i in range(size)]
        )

    fetched = {by: move(mine, by) for t in range(reach, 0, -1) for by in (t, -t)}
    blocks, steps = [], [0]
    for t in range(1, reach + 1):
        blocks += [fetched[t], fetched[-t]]
        steps += [-t, t]
    sends = [by for t in range(1, reach) for by in (t, -t)] + [-reach]
    steps += [-(by + reach) if by > 0 else reach - by for by in sends]

    place = jnp.where(device % 2 == 0, device // 2, size - 1 - device // 2)
    where = (place + jnp.array(steps, jnp.int32)) % size
    where = jnp.where(where < size // 2, 2 * where, 2 * (size - 1 - where) + 1)

    held = 2 * reach - 1
    early, lefts = pl.pallas_call(
        early_gram,
        out_shape=(
            jax.ShapeDtypeStruct((held, width, width), jnp.float32),
            jax.ShapeDtypeStruct((held, width, rows), mine.dtype),
        ),
        in_specs=[VMEM] * held,
        out_specs=(VMEM, VMEM),
        compiler_params=params(16),
    )(mine, *blocks[:-2])
    message = jax.ShapeDtypeStruct((width + share, width), mine.dtype)
    messages = pl.pallas_call(
        far_messages,
        out_shape=(message,) * len(sends),
        in_specs=[SMEM] + [VMEM] * 3,
        out_specs=(VMEM,) * len(sends),
        compiler_params=params(16),
    )(where, lefts, *blocks[-2:])
    own = pl.pallas_call(
        own_blocks,
        out_shape=jax.ShapeDtypeStruct((held + 2, width, width), jnp.float32),
        in_specs=[VMEM] * 4 + [ANY],
        out_specs=VMEM,
        compiler_params=params(16),
    )(lefts, early, *blocks[-2:], messages[-1])
    messages = [move(value, by) for value, by in zip(messages, sends)]
    own, messages = lax.optimization_barrier((sum_of_cores(own), messages))
    far = jnp.stack([message[:width] for message in messages]).astype(jnp.float32)

    flat = width % 128 == 0
    shape = (lambda n: (n, size * width)) if flat else (lambda n: (size, n, width))
    far, messages = lax.optimization_barrier((sum_of_cores(far), messages))
    rowwise = pl.pallas_call(
        functools.partial(filtered_rows, len(blocks)),
        out_shape=jax.ShapeDtypeStruct(shape(share), mine.dtype),
        in_specs=[SMEM] + [VMEM] * (1 + len(blocks) + len(messages)),
        out_specs=VMEM,
        compiler_params=params(16),
    )(where, mine, *blocks, *messages)
    own, _ = sum_of_chips(own)
    far, rowwise = sum_of_chips(far, rowwise)
    gram = pl.pallas_call(
        functools.partial(place_blocks, 1.0 / (rows * lax.axis_size("rows"))),
        out_shape=jax.ShapeDtypeStruct(shape(width), jnp.float32),
        in_specs=[SMEM] * 2 + [VMEM] * 4,
        out_specs=VMEM,
        compiler_params=params(16),
    )(where, (lax.axis_index("rows") & 1)[None], own, with_core(own), far, with_core(far))
    if not flat:
        gram = gram.transpose(1, 0, 2).reshape(width, size * width)
        rowwise = rowwise.transpose(1, 0, 2).reshape(share, size * width)
    return rowwise, gram


def sum_of_cores(blocks):
    odd = lax.axis_index("rows") & 1
    half = blocks.shape[1] // 2
    keep = lax.dynamic_slice_in_dim(blocks, odd * half, half, 1)
    give = lax.dynamic_slice_in_dim(blocks, (1 - odd) * half, half, 1)
    return (keep + with_core(give)).astype(jnp.bfloat16)


def sum_of_chips(sent, beside=None):
    size = lax.axis_size("rows")
    total = sent.astype(jnp.float32)
    bit = 2
    while bit < size:
        got = lax.ppermute(sent, "rows", [(i, i ^ bit) for i in range(size)])
        if beside is not None:
            got, beside = lax.optimization_barrier((got, beside))
        total = sent.astype(jnp.float32) + got.astype(jnp.float32)
        sent = total.astype(jnp.bfloat16)
        bit *= 2
    return total, beside


def per_device(search_vectors, tile_values, block_columns):
    row_part = lax.axis_index("rows")
    col_parts = lax.axis_size("cols")
    count, tile, depth = tile_values.shape
    kt = block_columns.shape[1]
    assert REACH == count
    share = search_vectors.shape[0]
    width = search_vectors.shape[1] // col_parts
    rows = share * col_parts
    second = with_chip(tile_values)
    columns = lax.all_to_all(search_vectors, "cols", split_axis=1, concat_axis=0, tiled=True)

    size = HALO * tile
    odd = row_part & 1
    block_columns = block_columns.T
    inner = jnp.arange(count, dtype=jnp.int32)

    offsets = block_columns - (row_part * count + inner)

    scratch = [
        pltpu.VMEM((HALO, kt + 1, tile, 2 * tile), jnp.bfloat16),
        pltpu.SMEM((HALO, 2 * HALO + 1), jnp.int32),
    ]
    bands, to_first, sent_offsets = pl.pallas_call(
        own_bands,
        out_shape=(
            jax.ShapeDtypeStruct((count // HALO, size, SPAN * size), jnp.bfloat16),
            jax.ShapeDtypeStruct((TILES_REACH, tile, depth), jnp.bfloat16),
            jax.ShapeDtypeStruct((kt, count), jnp.int32),
        ),
        in_specs=[SMEM, SMEM, VMEM, VMEM],
        out_specs=(VMEM,) * 3,
        scratch_shapes=scratch,
        compiler_params=params(16),
    )(odd[None], offsets, offsets, tile_values)
    first = with_core(to_first)
    at_first = with_core(sent_offsets)
    at_second = with_chip(sent_offsets)
    edges = pl.pallas_call(
        edge_bands,
        out_shape=jax.ShapeDtypeStruct(
            (2 * TILES_REACH // HALO, size, SPAN * size), jnp.bfloat16
        ),
        in_specs=[SMEM] * 3 + [VMEM] * 2,
        out_specs=VMEM,
        scratch_shapes=scratch,
        compiler_params=params(16),
    )(
        odd[None],
        jnp.clip(at_first, -HALO, HALO),
        jnp.clip(at_second, -HALO, HALO),
        first,
        second,
    )
    x_second = with_chip(columns)
    x_first = with_core(columns)

    window = [
        pltpu.VMEM((3 * rows, width), dtype)
        for dtype in (jnp.bfloat16, jnp.bfloat16, jnp.float32, jnp.float32)
    ]
    now, last, sent = pl.pallas_call(
        first_stage,
        out_shape=(
            jax.ShapeDtypeStruct((rows, width), jnp.float32),
            jax.ShapeDtypeStruct((rows + 2 * size, width), jnp.float32),
            jax.ShapeDtypeStruct((2 * rows - 2 * size, width), jnp.bfloat16),
        ),
        in_specs=[SMEM] + [VMEM] * 5,
        out_specs=(VMEM,) * 3,
        scratch_shapes=window,
        compiler_params=params(24),
    )(odd[None], bands, edges, x_first, columns, x_second)
    got_second = with_chip(sent)
    got_first = with_core(sent)
    filtered = pl.pallas_call(
        second_stage,
        out_shape=jax.ShapeDtypeStruct((rows, width), jnp.bfloat16),
        in_specs=[SMEM] + [VMEM] * 6,
        out_specs=VMEM,
        scratch_shapes=window,
        compiler_params=params(24),
    )(odd[None], bands, edges, now, last, got_first, got_second)

    return gram_and_rows(filtered)


def solution(mesh):
    return jax.shard_map(
        per_device,
        mesh=mesh,
        in_specs=(P(("rows", "cols"), None), P("rows", None, None), P("rows", None)),
        out_specs=(P(("rows", "cols"), None), P("cols", None)),
        check_vma=False,
    )
```

```python
import functools

import functools

import jax
import jax.numpy as jnp
from jax import lax
from jax.experimental import pallas as pl
from jax.experimental.pallas import tpu as pltpu
from jax.sharding import PartitionSpec as P

HALO = 4
DEGREE = 8
STAGE = 4
REACH = HALO * STAGE
TILES_REACH = REACH - HALO
SPAN = 3

shift_value = 0.1
half_width = 2.0

SMEM = pl.BlockSpec(memory_space=pltpu.SMEM)
VMEM = pl.BlockSpec(memory_space=pltpu.VMEM)
ANY = pl.BlockSpec(memory_space=pl.ANY)


def params(mebibytes):
    return pltpu.CompilerParams(vmem_limit_bytes=mebibytes * 1024 * 1024)


def with_core(value):
    return lax.ppermute(value, "rows", [(i, i ^ 1) for i in range(lax.axis_size("rows"))])


def with_chip(value):
    odds = range(1, lax.axis_size("rows") - 1, 2)
    return lax.ppermute(value, "rows", [p for k in odds for p in ((k, k + 1), (k + 1, k))])


def place_group(offsets, ahead, tiles, start, bands, band, doubled, slot):
    kt = offsets.shape[0]
    tile = tiles.shape[1]
    blank = kt
    nothing = jnp.zeros((tile, tile), doubled.dtype)
    for i in range(HALO):
        values = tiles[start + i]
        for k in range(kt):
            one = values[:, k * tile:(k + 1) * tile]
            doubled[i, k] = jnp.concatenate([one, one], axis=1)
        for place in range(2 * HALO + 1):
            slot[i, place] = blank
        for k in range(kt):
            slot[i, offsets[k, ahead + start + i] + HALO] = k
    for i in range(HALO):
        rows = slice(i * tile, (i + 1) * tile)
        for pair in range(SPAN * HALO // 2):
            halves = []
            for side in range(2):
                place = 2 * pair + side - i
                if 0 <= place <= 2 * HALO:
                    both = doubled[i, slot[i, place]]
                    halves.append(both[:, side * tile:(side + 1) * tile])
                else:
                    halves.append(nothing)
            columns = slice(2 * pair * tile, 2 * (pair + 1) * tile)
            bands[band, rows, columns] = jnp.concatenate(halves, axis=1)


def clear(doubled):
    doubled[:, doubled.shape[1] - 1] = jnp.zeros(
        doubled.shape[:1] + doubled.shape[2:], doubled.dtype
    )


def place_group(offsets, ahead, tiles, start, bands, band, doubled, slot):
    kt = offsets.shape[0]
    tile = tiles.shape[1]
    blank = kt
    nothing = jnp.zeros((tile, tile), doubled.dtype)
    for i in range(HALO):
        values = tiles[start + i]
        for k in range(kt):
            one = values[:, k * tile:(k + 1) * tile]
            doubled[i, k] = jnp.concatenate([one, one], axis=1)
        for place in range(2 * HALO + 1):
            slot[i, place] = blank
        for k in range(kt):
            slot[i, offsets[k, ahead + start + i] + HALO] = k
    for i in range(HALO):
        rows = slice(i * tile, (i + 1) * tile)
        for pair in range(SPAN * HALO // 2):
            halves = []
            for side in range(2):
                place = 2 * pair + side - i
                if 0 <= place <= 2 * HALO:
                    both = doubled[i, slot[i, place]]
                    halves.append(both[:, side * tile:(side + 1) * tile])
                else:
                    halves.append(nothing)
            columns = slice(2 * pair * tile, 2 * (pair + 1) * tile)
            bands[band, rows, columns] = jnp.concatenate(halves, axis=1)


def clear(doubled):
    doubled[:, doubled.shape[1] - 1] = jnp.zeros(
        doubled.shape[:1] + doubled.shape[2:], doubled.dtype
    )


def split_columns(vectors, pieces):
    width = pieces.shape[2]
    for i in range(pieces.shape[0]):
        pieces[i] = vectors[:, i * width:(i + 1) * width]


def copy_columns(vectors, pieces, done):
    width = pieces.shape[2]
    copies = [
        pltpu.make_async_copy(
            vectors.at[:, i * width:(i + 1) * width], pieces.at[i], done.at[i]
        )
        for i in range(pieces.shape[0])
    ]
    for copy in copies:
        copy.start()
    for copy in copies:
        copy.wait()


def own_bands(odd, offsets, to_send, tiles, bands, to_first, offsets_out, doubled, slot):
    count = tiles.shape[0]
    sent = to_first.shape[0]
    to_first[...] = tiles[pl.ds((1 - odd[0]) * (count - sent), sent)]
    offsets_out[...] = to_send[...]
    clear(doubled)

    @pl.loop(0, count // HALO)
    def _(g):
        place_group(offsets, 0, tiles, g * HALO, bands, g, doubled, slot)


def edge_bands(odd, at_first, at_second, first, second, bands, doubled, slot):
    count = at_first.shape[1]
    edge = TILES_REACH // HALO
    clear(doubled)
    for offsets, tiles, behind in ((at_first, first, odd[0]), (at_second, second, 1 - odd[0])):
        begin = behind * (count - TILES_REACH)
        band = (1 - behind) * edge
        skipped = begin * (tiles.shape[0] // count)

        @pl.loop(0, edge)
        def _(g, offsets=offsets, tiles=tiles, begin=begin, band=band, skipped=skipped):
            place_group(offsets, begin - skipped, tiles, skipped + g * HALO, bands, band + g,
                        doubled, slot)


def run_steps(own, edges, w, y, degree, now=None):
    middle, size, span = own.shape
    edge = edges.shape[0] // 2
    bands = [edges.at[j] for j in range(edge)]
    bands += [own.at[j] for j in range(middle)]
    bands += [edges.at[edge + j] for j in range(edge)]
    groups = len(bands)
    cur, new = y
    src, dst = w
    for step in range(STAGE):
        for j in range(step, groups - step):
            start = j * size
            here = slice(start + size, start + 2 * size)
            product = dot(bands[j][...], src[start:start + span])
            k = j - edge
            mine = now is not None and 0 <= k < middle
            given = src if step == 0 else dst
            start_value = (
                now[k * size:(k + 1) * size] if mine else given[here].astype(jnp.float32)
            )
            value = product - shift_value * (start_value if step == 0 else cur[here])
            if degree + step == 0:
                value = value / half_width
            else:
                value = value - (start_value if step == 1 else new[here])
            new[here] = value
            dst[here] = value.astype(jnp.bfloat16)
        cur, new = new, cur
        src, dst = dst, src
    return cur, new, src


def placed(behind, rows):
    return pl.multiple_of((1 - behind) * 2 * rows, rows)


def first_stage(odd, own, edges, x_first, x_own, x_second, now_out, last_out, sent_out,
                w0, w1, y0, y1):
    rows = x_own.shape[0]
    size = own.shape[1]
    starts = (placed(odd[0], rows), rows, placed(1 - odd[0], rows))
    for start, ref in zip(starts, (x_first, x_own, x_second)):
        w0[pl.ds(start, rows)] = ref[...]
    cur, prev, rounded = run_steps(own, edges, (w0, w1), (y0, y1), 0)
    now_out[...] = cur[rows:2 * rows]
    last_out[...] = prev[rows - size:2 * rows + size]
    sent_out[:rows] = rounded[rows:2 * rows]
    sent_out[rows:] = prev[rows + size:2 * rows - size].astype(jnp.bfloat16)


def second_stage(odd, own, edges, now, last, got_first, got_second, out, w0, w1, y0, y1):
    rows = now.shape[0]
    size = own.shape[1]
    here = slice(rows, 2 * rows)
    w0[here] = now[...].astype(jnp.bfloat16)
    y1[rows - size:2 * rows + size] = last[...]
    for got, behind in ((got_first, odd[0]), (got_second, 1 - odd[0])):
        start = placed(behind, rows)
        w0[pl.ds(start, rows)] = got[:rows]
        y1[pl.ds(pl.multiple_of(start + size, size), rows - 2 * size)] = (
            got[rows:].astype(jnp.float32)
        )
    _, _, rounded = run_steps(own, edges, (w0, w1), (y0, y1), STAGE, now)
    out[...] = rounded[here]


def dot(a, b):
    return jnp.dot(a, b, preferred_element_type=jnp.float32)


def columns_at(ref, group, width):
    if len(ref.shape) == 2:
        return slice(None), pl.ds(pl.multiple_of(group * width, width), width)
    return (group,)


def early_gram(mine, *refs):
    *blocks, partial, lefts = refs
    left = mine[...].T
    lefts[0] = left
    for t, ref in enumerate((mine, *blocks)):
        block = ref[...]
        if t:
            lefts[t] = block.T
        partial[t] = dot(left, block)


def far_messages(where, lefts, back, front, *messages):
    width = lefts.shape[1]
    share = messages[0].shape[0] - width
    reach = lefts.shape[0] // 2 + 1
    far_back, far_front = back[...], front[...]
    made = []
    for t in range(1, reach):
        made.append((dot(lefts[2 * t], far_back), back, where[2 * t]))
        made.append((dot(lefts[2 * t - 1], far_front), front, where[2 * t - 1]))
    made.append((dot(far_back.T, far_front), front, where[2 * reach - 1]))
    for message, (block, source, device) in zip(messages, made):
        message[:width] = block.astype(message.dtype)
        message[width:] = source[pl.ds(pl.multiple_of(device * share, share), share)]


def own_blocks(lefts, early, back, front, _, partial):
    held = early.shape[0]
    partial[:held] = early[...]
    partial[held] = dot(lefts[0], back[...])
    partial[held + 1] = dot(lefts[0], front[...])


def place_blocks(scale, where, odd, *refs):
    own, own_other, far, far_other, gram = refs
    half, width = own.shape[1:]
    first = own.shape[0]
    for side, (near, distant) in enumerate(((own, far), (own_other, far_other))):
        rows = pl.ds(pl.multiple_of((odd[0] ^ side) * half, half), half)
        for t in range(first + far.shape[0]):
            block = near[t] if t < first else distant[t - first]
            if len(gram.shape) == 2:
                start = pl.multiple_of(where[t] * width, width)
                gram[rows, pl.ds(start, width)] = block * scale
            else:
                gram[where[t], rows] = block * scale


def filtered_rows(number, where, mine, *refs):
    blocks, messages, rowwise = (mine,) + refs[:number], refs[number:-1], refs[-1]
    width = mine.shape[1]
    share = rowwise.shape[-2]
    start = pl.multiple_of(where[0] * share, share)
    for t, block in enumerate(blocks):
        rowwise[columns_at(rowwise, where[t], width)] = block[pl.ds(start, share)]
    for t, message in enumerate(messages):
        rowwise[columns_at(rowwise, where[1 + number + t], width)] = message[width:]


def ring_of(size):
    return list(range(0, size, 2)) + list(range(size - 1, 0, -2))


def gram_and_rows(mine):
    size = lax.axis_size("cols")
    device = lax.axis_index("cols")
    assert size % 4 == 0
    reach = size // 4
    order = ring_of(size)
    rows, width = mine.shape
    share = rows // size

    def move(value, by):
        return lax.ppermute(
            value, "cols", [(order[i], order[(i + by) % size]) for i in range(size)]
        )

    fetched = {by: move(mine, by) for t in range(reach, 0, -1) for by in (t, -t)}
    blocks, steps = [], [0]
    for t in range(1, reach + 1):
        blocks += [fetched[t], fetched[-t]]
        steps += [-t, t]
    sends = [by for t in range(1, reach) for by in (t, -t)] + [-reach]
    steps += [-(by + reach) if by > 0 else reach - by for by in sends]

    place = jnp.where(device % 2 == 0, device // 2, size - 1 - device // 2)
    where = (place + jnp.array(steps, jnp.int32)) % size
    where = jnp.where(where < size // 2, 2 * where, 2 * (size - 1 - where) + 1)

    held = 2 * reach - 1
    early, lefts = pl.pallas_call(
        early_gram,
        out_shape=(
            jax.ShapeDtypeStruct((held, width, width), jnp.float32),
            jax.ShapeDtypeStruct((held, width, rows), mine.dtype),
        ),
        in_specs=[VMEM] * held,
        out_specs=(VMEM, VMEM),
        compiler_params=params(16),
    )(mine, *blocks[:-2])
    message = jax.ShapeDtypeStruct((width + share, width), mine.dtype)
    messages = pl.pallas_call(
        far_messages,
        out_shape=(message,) * len(sends),
        in_specs=[SMEM] + [VMEM] * 3,
        out_specs=(VMEM,) * len(sends),
        compiler_params=params(16),
    )(where, lefts, *blocks[-2:])
    own = pl.pallas_call(
        own_blocks,
        out_shape=jax.ShapeDtypeStruct((held + 2, width, width), jnp.float32),
        in_specs=[VMEM] * 4 + [ANY],
        out_specs=VMEM,
        compiler_params=params(16),
    )(lefts, early, *blocks[-2:], messages[-1])
    messages = [move(value, by) for value, by in zip(messages, sends)]
    own, messages = lax.optimization_barrier((sum_of_cores(own), messages))
    far = jnp.stack([message[:width] for message in messages]).astype(jnp.float32)

    flat = width % 128 == 0
    shape = (lambda n: (n, size * width)) if flat else (lambda n: (size, n, width))
    far = sum_of_cores(far)
    rowwise = pl.pallas_call(
        functools.partial(filtered_rows, len(blocks)),
        out_shape=jax.ShapeDtypeStruct(shape(share), mine.dtype),
        in_specs=[SMEM] + [VMEM] * (1 + len(blocks) + len(messages)),
        out_specs=VMEM,
        compiler_params=params(16),
    )(where, mine, *blocks, *messages)
    own = sum_of_chips(own)
    far = sum_of_chips(far)
    gram = pl.pallas_call(
        functools.partial(place_blocks, 1.0 / (rows * lax.axis_size("rows"))),
        out_shape=jax.ShapeDtypeStruct(shape(width), jnp.float32),
        in_specs=[SMEM] * 2 + [VMEM] * 4,
        out_specs=VMEM,
        compiler_params=params(16),
    )(where, (lax.axis_index("rows") & 1)[None], own, with_core(own), far, with_core(far))
    if not flat:
        gram = gram.transpose(1, 0, 2).reshape(width, size * width)
        rowwise = rowwise.transpose(1, 0, 2).reshape(share, size * width)
    return rowwise, gram


def sum_of_cores(blocks):
    odd = lax.axis_index("rows") & 1
    half = blocks.shape[1] // 2
    keep = lax.dynamic_slice_in_dim(blocks, odd * half, half, 1)
    give = lax.dynamic_slice_in_dim(blocks, (1 - odd) * half, half, 1)
    return (keep + with_core(give)).astype(jnp.bfloat16)


def sum_of_chips(sent):
    size = lax.axis_size("rows")
    total = sent.astype(jnp.float32)
    bit = 2
    while bit < size:
        got = lax.ppermute(sent, "rows", [(i, i ^ bit) for i in range(size)])
        total = sent.astype(jnp.float32) + got.astype(jnp.float32)
        sent = total.astype(jnp.bfloat16)
        bit *= 2
    return total


def per_device(search_vectors, tile_values, block_columns):
    row_part = lax.axis_index("rows")
    col_parts = lax.axis_size("cols")
    count, tile, depth = tile_values.shape
    kt = block_columns.shape[1]
    assert REACH == count
    share = search_vectors.shape[0]
    width = search_vectors.shape[1] // col_parts
    rows = share * col_parts
    second = with_chip(tile_values)
    columns = lax.all_to_all(search_vectors, "cols", split_axis=1, concat_axis=0, tiled=True)

    size = HALO * tile
    odd = row_part & 1
    block_columns = block_columns.T
    inner = jnp.arange(count, dtype=jnp.int32)

    offsets = block_columns - (row_part * count + inner)

    scratch = [
        pltpu.VMEM((HALO, kt + 1, tile, 2 * tile), jnp.bfloat16),
        pltpu.SMEM((HALO, 2 * HALO + 1), jnp.int32),
    ]
    bands, to_first, sent_offsets = pl.pallas_call(
        own_bands,
        out_shape=(
            jax.ShapeDtypeStruct((count // HALO, size, SPAN * size), jnp.bfloat16),
            jax.ShapeDtypeStruct((TILES_REACH, tile, depth), jnp.bfloat16),
            jax.ShapeDtypeStruct((kt, count), jnp.int32),
        ),
        in_specs=[SMEM, SMEM, VMEM, VMEM],
        out_specs=(VMEM,) * 3,
        scratch_shapes=scratch,
        compiler_params=params(16),
    )(odd[None], offsets, offsets, tile_values)
    first = with_core(to_first)
    at_first = with_core(sent_offsets)
    at_second = with_chip(sent_offsets)
    edges = pl.pallas_call(
        edge_bands,
        out_shape=jax.ShapeDtypeStruct(
            (2 * TILES_REACH // HALO, size, SPAN * size), jnp.bfloat16
        ),
        in_specs=[SMEM] * 3 + [VMEM] * 2,
        out_specs=VMEM,
        scratch_shapes=scratch,
        compiler_params=params(16),
    )(
        odd[None],
        jnp.clip(at_first, -HALO, HALO),
        jnp.clip(at_second, -HALO, HALO),
        first,
        second,
    )
    x_second = with_chip(columns)
    x_first = with_core(columns)

    window = [
        pltpu.VMEM((3 * rows, width), dtype)
        for dtype in (jnp.bfloat16, jnp.bfloat16, jnp.float32, jnp.float32)
    ]
    now, last, sent = pl.pallas_call(
        first_stage,
        out_shape=(
            jax.ShapeDtypeStruct((rows, width), jnp.float32),
            jax.ShapeDtypeStruct((rows + 2 * size, width), jnp.float32),
            jax.ShapeDtypeStruct((2 * rows - 2 * size, width), jnp.bfloat16),
        ),
        in_specs=[SMEM] + [VMEM] * 5,
        out_specs=(VMEM,) * 3,
        scratch_shapes=window,
        compiler_params=params(24),
    )(odd[None], bands, edges, x_first, columns, x_second)
    got_second = with_chip(sent)
    got_first = with_core(sent)
    filtered = pl.pallas_call(
        second_stage,
        out_shape=jax.ShapeDtypeStruct((rows, width), jnp.bfloat16),
        in_specs=[SMEM] + [VMEM] * 6,
        out_specs=VMEM,
        scratch_shapes=window,
        compiler_params=params(24),
    )(odd[None], bands, edges, now, last, got_first, got_second)

    return gram_and_rows(filtered)


def solution(mesh):
    return jax.shard_map(
        per_device,
        mesh=mesh,
        in_specs=(P(("rows", "cols"), None), P("rows", None, None), P("rows", None)),
        out_specs=(P(("rows", "cols"), None), P("cols", None)),
        check_vma=False,
    )
```
